32 devices in a mesh: member: 4 (over y, x), lat: 8 (over z, core).
Axes of the slice: x: 2, y: 2, z: 4, core: 2. Of those that a mesh axis runs over, the one named last changes fastest.
Arguments:
- state_now: float32 [8, 96, 180, 633], P('member', 'lat'), may hold values from -6 to 6
- sample_random_maps: float32 [8, 96, 180, 8], P('member', 'lat'), may hold values from -6 to 6
- noise_scale: float32 [8, 8], P('member'), may hold values from 0.2 to 2
- spec_gain: float32 [91, 641], replicated, may hold values from 0.2 to 1.8
- weight_in: float32 [641, 1282], replicated, may hold values from -0.25 to 0.25
- bias_in: float32 [1282], replicated, may hold values from -3 to 3
- weight_out: float32 [1282, 641], replicated, may hold values from -0.15625 to 0.15625
- bias_out: float32 [641], replicated, may hold values from -3 to 3
- targets: float32 [2, 96, 180, 633], P(None, 'lat'), may hold values from -6 to 6
- date_of: int32 [8], replicated, may hold values from 0 to 1, as said below
- row_slot: int32 [90], replicated, may hold values from 0 to 95, as said below
Outputs:
- crps_loss: float32 [], replicated
- layer_output: float32 [8, 96, 180, 641], P('member', 'lat')
- grad_state: float32 [8, 96, 180, 633], P('member', 'lat')
- grad_scale: float32 [8, 8], P('member')
- grad_gain: float32 [91, 641], replicated
- grad_weight_in: float32 [641, 1282], replicated
- grad_bias_in: float32 [1282], replicated
- grad_weight_out: float32 [1282, 641], replicated
- grad_bias_out: float32 [641], replicated
The draws below stay inside these ranges and needn't reach their ends.
Inputs may be any that keep to these rules, and one draw needn't show every extreme that they name: `date_of`: each of the 2 dates is named by exactly 4 members. `row_slot`: strictly increasing, north to south; slot s lies on lat index s // 12; the first and the last lat index hold 12 rows each.
All inputs are finite; a program needn't handle non-finite values.
Results may differ from the reference program's by a relative error of at most 0.0003.
Values sent between devices are 32-bit elements; how exact they have to be, the bound alone decides.
A program may use at most 384 MiB of HBM per device.

```python
import math
from functools import partial
import jax
import jax.numpy as jnp
from jax import lax

VARIABLE_COUNT = 633
NN = 8
C = 641
HID = 1282
LMAX = 90
NLAT = 90
NLON = 180
ENSEMBLE_SIZE = 4
DATES = 2
MEMBERS = 8
ROWS_DEV = 12
SLOTS = 96


def draw_date_of(key, part):
    key = jax.random.fold_in(key, 11)
    base_dates = jnp.arange(MEMBERS, dtype=jnp.int32) // ENSEMBLE_SIZE
    return jax.random.permutation(key, base_dates).astype(jnp.int32)


def draw_row_slot(key, part):
    key = jax.random.fold_in(key, 23)
    device_count = SLOTS // ROWS_DEV
    chosen_key, score_key = jax.random.split(key)
    chosen = jax.random.randint(chosen_key, (), 1, device_count - 1)
    scores = jax.random.randint(score_key, (SLOTS,), 0, 1 << 20)
    owner = jnp.arange(SLOTS, dtype=jnp.int32) // ROWS_DEV
    forced = (owner == 0) | (owner == device_count - 1) | (owner == chosen)
    scores = jnp.where(forced, -1, scores)
    ranking = jnp.argsort(scores, stable=True)
    return jnp.sort(ranking[:NLAT]).astype(jnp.int32)


def block_levels(stream_key, dims, cuts, smallest, largest):
    def one(axis_at, parts):
        draws = jax.random.uniform(jax.random.fold_in(jax.random.fold_in(stream_key, 6), axis_at), (parts,), jnp.float32, smallest / len(cuts), largest / len(cuts))
        return jnp.repeat(jnp.exp(draws), dims[axis_at] // parts).reshape((-1,) + (1,) * (len(dims) - axis_at - 1))

    level = one(*cuts[0])
    for cut in cuts[1:]:
        level = level * one(*cut)
    return level


def bell_draw(stream_key, shape, spread, most, cuts=(), held_as=jnp.bfloat16):
    array = jax.random.normal(stream_key, shape, jnp.float32) * spread
    if len(cuts) > 0:
        array = block_levels(stream_key, shape, cuts, -0.22, 0.18) * array
    return jnp.clip(array, min=-most, max=most).astype(held_as)


def setup_inputs(seed: int = 0) -> dict:
    seeds = jax.random.split(jax.random.key(seed), 12)
    state_now = bell_draw(seeds[0], (MEMBERS, SLOTS, NLON, VARIABLE_COUNT), 1.0, 6.0, ((0, 4), (1, 8)), jnp.float32)
    sample_random_maps = bell_draw(seeds[1], (MEMBERS, SLOTS, NLON, NN), 1.0, 6.0, ((0, 4), (1, 8)), jnp.float32)
    noise_scale = jnp.clip(jnp.exp(math.log(2.0) - 2.3025851 * jax.random.uniform(seeds[2], (MEMBERS, NN), jnp.float32) ** block_levels(seeds[2], (MEMBERS, NN), ((0, 4),), -0.2, 0.2)), 0.2, 2.0)
    spec_gain = jnp.clip(jax.random.uniform(seeds[3], (LMAX + 1, C), jnp.float32, 0.2, 1.8), 0.2, 1.8)
    weight_in = bell_draw(seeds[4], (C, HID), C ** -0.5, 0.25, (), jnp.float32)
    bias_in = bell_draw(seeds[5], (HID,), 0.5, 3.0, (), jnp.float32)
    weight_out = bell_draw(seeds[6], (HID, C), HID ** -0.5, 0.15625, (), jnp.float32)
    bias_out = bell_draw(seeds[7], (C,), 0.5, 3.0, (), jnp.float32)
    targets = bell_draw(seeds[8], (DATES, SLOTS, NLON, VARIABLE_COUNT), 1.0, 6.0, ((1, 8),), jnp.float32)
    date_of = draw_date_of(jax.random.fold_in(seeds[11], 71), 0)
    row_slot = draw_row_slot(jax.random.fold_in(seeds[11], 71), 0)
    return {"state_now": state_now, "sample_random_maps": sample_random_maps, "noise_scale": noise_scale, "spec_gain": spec_gain, "weight_in": weight_in, "bias_in": bias_in, "weight_out": weight_out, "bias_out": bias_out, "targets": targets, "date_of": date_of, "row_slot": row_slot}


@jax.custom_vjp
def low(v):
    return lax.optimization_barrier(v.astype(jnp.bfloat16)).astype(jnp.float32)

@jax.custom_vjp
def low_back(v):
    return v

def low_keep(v):
    return (low(v), None)

def low_pass(kept, grad):
    return (grad,)

def back_keep(v):
    return (v, None)

def back_low(kept, grad):
    return (low(grad),)
low.defvjp(low_keep, low_pass)
low_back.defvjp(back_keep, back_low)

def legendre(colatitude, orders):
    cosine = jnp.cos(colatitude)[None, :]
    log_sine = jnp.log(jnp.sin(colatitude))[None, :]
    order_col = orders[:, None]
    log_start = 0.5 * (jnp.log(2.0 * order_col + 1.0) - math.log(4.0 * math.pi) + lax.lgamma(order_col + 0.5) - 0.5 * math.log(math.pi) - lax.lgamma(order_col + 1.0)) + order_col * log_sine
    start_value = jnp.exp(log_start)
    blank_rows = jnp.zeros((orders.shape[0], colatitude.shape[0]), jnp.float32)

    def degree_step(carry, degree):
        latest, earlier = carry
        degree_value = degree.astype(jnp.float32)
        previous = degree_value - 1.0
        factor = jnp.sqrt((4.0 * degree_value * degree_value - 1.0) / jnp.maximum(degree_value * degree_value - order_col * order_col, 1.0))
        shrink = jnp.sqrt(jnp.maximum(previous * previous - order_col * order_col, 0.0) / jnp.maximum(4.0 * previous * previous - 1.0, 1.0))
        recursed = factor * (cosine * latest - shrink * earlier)
        newest = jnp.where(degree_value < order_col, 0.0, jnp.where(degree_value == order_col, start_value, recursed))
        return ((newest, latest), newest)
    _, stacked = lax.scan(degree_step, (blank_rows, blank_rows), jnp.arange(LMAX + 1, dtype=jnp.int32))
    return jnp.transpose(stacked, (1, 0, 2))

def fourier_tables(lon_count, wave_count):
    column = jnp.arange(lon_count, dtype=jnp.int32)[:, None]
    wave = jnp.arange(wave_count, dtype=jnp.int32)[None, :]
    phase = column * wave % lon_count
    angle = 2.0 * math.pi / lon_count * phase.astype(jnp.float32)
    keeping = (wave <= LMAX).astype(jnp.float32)
    basis = jnp.stack([jnp.cos(angle) * keeping, -jnp.sin(angle) * keeping], axis=-1)
    doubling = jnp.where((wave == 0) | (2 * wave == lon_count), 1.0, 2.0).astype(jnp.float32)
    return (basis * (2.0 * math.pi / lon_count), basis * doubling[:, :, None])

def softened_modulus(value):
    return jnp.sqrt(value * value + 1.0)

def reference(state_now, sample_random_maps, noise_scale, spec_gain, weight_in, bias_in, weight_out, bias_out, targets, date_of, row_slot):
    highest = lax.Precision.HIGHEST
    lat_ids = jnp.arange(NLAT, dtype=jnp.int32)
    colatitude = (lat_ids.astype(jnp.float32) + 0.5) * (math.pi / NLAT)
    sine_rows = jnp.sin(colatitude)
    quadrature = math.pi / NLAT * sine_rows
    area_weight = NLAT * sine_rows / jnp.sum(sine_rows)
    legendre_table = legendre(colatitude, jnp.arange(LMAX + 1, dtype=jnp.int32).astype(jnp.float32))
    weighted_table = legendre_table * quadrature[None, None, :]
    forward_table, inverse_table = fourier_tables(NLON, LMAX + 1)
    groups = jnp.argsort(date_of, stable=True).astype(jnp.int32).reshape(DATES, ENSEMBLE_SIZE)
    state_rows = jnp.take(state_now, row_slot, axis=1)
    noise_rows = jnp.take(sample_random_maps, row_slot, axis=1)
    target_rows = jnp.take(targets, row_slot, axis=1)

    def date_total(state_part, scale_part, gain, first_weight, first_bias, second_weight, second_bias, noise_part, observed_latitude_entries):
        inputs = jnp.concatenate([state_part, scale_part[:, None, None, :] * noise_part], axis=-1)
        spectral_in = jnp.einsum('bjkc,kmp->bjmpc', inputs, forward_table, precision=highest)
        coeffs = jnp.einsum('mlj,bjmpc->blmpc', weighted_table, spectral_in, precision=highest)
        filtered = coeffs * gain[None, :, None, None, :]
        synthesis = jnp.einsum('mlj,blmpc->bjmpc', legendre_table, filtered, precision=highest)
        smooth = jnp.einsum('bjmpc,kmp->bjkc', synthesis, inverse_table, precision=highest)
        mixed_rows = inputs + smooth
        hidden_pre = jnp.einsum('bjkc,ch->bjkh', mixed_rows, first_weight, precision=highest) + first_bias
        activated = jax.nn.gelu(hidden_pre, approximate=False)
        layer_latitude_entries = mixed_rows + jnp.einsum('bjkh,hc->bjkc', activated, second_weight, precision=highest) + second_bias
        sample_prediction = layer_latitude_entries[..., :VARIABLE_COUNT]
        skill_component = lax.optimization_barrier(jnp.mean(softened_modulus(sample_prediction - observed_latitude_entries[None]), axis=0))
        couple_component = jnp.zeros_like(skill_component)
        for outer_dimensions in range(ENSEMBLE_SIZE):
            for inner_dimensions in range(outer_dimensions + 1, ENSEMBLE_SIZE):
                couple_component = couple_component + softened_modulus(sample_prediction[outer_dimensions] - sample_prediction[inner_dimensions])
        crps_rows = skill_component - couple_component / (ENSEMBLE_SIZE * (ENSEMBLE_SIZE - 1))
        return (jnp.sum(area_weight[:, None, None] * crps_rows), layer_latitude_entries)

    def one_date(carry, date_index):
        weight_sums, total_sum, block_all, state_grads, scale_grads = carry
        members = groups[date_index]
        primals = (jnp.take(state_rows, members, axis=0), jnp.take(noise_scale, members, axis=0), spec_gain, weight_in, bias_in, weight_out, bias_out)
        bound_total = partial(date_total, noise_part=jnp.take(noise_rows, members, axis=0), observed_latitude_entries=target_rows[date_index])
        total_here, pull_back, layer_latitude_entries = jax.vjp(bound_total, *primals, has_aux=True)
        cotangents = pull_back(jnp.ones_like(total_here))
        weight_sums = tuple((acc + new for acc, new in zip(weight_sums, cotangents[2:])))
        block_all = block_all.at[members].set(layer_latitude_entries)
        state_grads = state_grads.at[members].set(cotangents[0])
        scale_grads = scale_grads.at[members].set(cotangents[1])
        return ((weight_sums, total_sum + total_here, block_all, state_grads, scale_grads), None)
    start_carry = ((jnp.zeros_like(spec_gain), jnp.zeros_like(weight_in), jnp.zeros_like(bias_in), jnp.zeros_like(weight_out), jnp.zeros_like(bias_out)), jnp.zeros((), jnp.float32), jnp.zeros((MEMBERS, NLAT, NLON, VARIABLE_COUNT + NN), jnp.float32), jnp.zeros((MEMBERS, NLAT, NLON, VARIABLE_COUNT), jnp.float32), jnp.zeros((MEMBERS, NN), jnp.float32))
    final_carry, _ = lax.scan(one_date, start_carry, jnp.arange(DATES, dtype=jnp.int32))
    weight_sums, total_sum, block_all, state_grads, scale_grads = final_carry
    layer_output = jnp.zeros((MEMBERS, SLOTS, NLON, VARIABLE_COUNT + NN), jnp.float32).at[:, row_slot].set(block_all)
    grad_state = jnp.zeros((MEMBERS, SLOTS, NLON, VARIABLE_COUNT), jnp.float32).at[:, row_slot].set(state_grads)
    crps_loss = total_sum / (DATES * NLAT * NLON * VARIABLE_COUNT)
    return (crps_loss, layer_output, grad_state, scale_grads, weight_sums[0], weight_sums[1], weight_sums[2], weight_sums[3], weight_sums[4])
```

```python
import functools
import math

import jax
import jax.numpy as jnp
import ml_dtypes
import numpy as np
from jax import lax
from jax.experimental import pallas as pl
from jax.experimental.pallas import tpu as pltpu
from jax.sharding import PartitionSpec as P

VARIABLE_COUNT = 633
LMAX = 90
NLAT = 90
NLON = 180
ENSEMBLE_SIZE = 4
DATES = 2

LANES = 128
VMEM_LIMIT = 56 * 1024 * 1024
F32 = jnp.float32
BF16 = jnp.bfloat16


def cost(microseconds):
    return pl.CostEstimate(
        flops=int(microseconds * 1.0e9), bytes_accessed=1000, transcendentals=0
    )


def legendre_np():
    colat = (np.arange(NLAT) + 0.5) * (math.pi / NLAT)
    cosine, log_sine = np.cos(colat), np.log(np.sin(colat))
    table = np.zeros((LMAX + 1, LMAX + 1, NLAT))
    for m in range(LMAX + 1):
        start = 0.5 * (
            math.log(2.0 * m + 1.0)
            - math.log(4.0 * math.pi)
            + math.lgamma(m + 0.5)
            - 0.5 * math.log(math.pi)
            - math.lgamma(m + 1.0)
        )
        table[m, m] = np.exp(start + m * log_sine)
        for l in range(m + 1, LMAX + 1):
            factor = math.sqrt((4.0 * l * l - 1.0) / (l * l - m * m))
            shrink = math.sqrt(((l - 1.0) ** 2 - m * m) / (4.0 * (l - 1.0) ** 2 - 1.0))
            before = table[m, l - 2] if l >= m + 2 else 0.0
            table[m, l] = factor * (cosine * table[m, l - 1] - shrink * before)
    return table


def unit_plan(devices):
    whole = LMAX // 2 * 2 - 1
    rows = 8
    while True:
        pairs = rows // 2 - 1
        left = max(0, whole - devices * pairs)
        if 2 + 2 * left <= devices:
            break
        rows += 8
    orders = np.zeros((devices, rows // 2), np.int32)
    units = {}
    for i in range(whole - left):
        d, j = i % devices, i // devices
        orders[d, j] = i + 1
        units[d * rows + 2 * j] = (i + 1, 0)
        units[d * rows + 2 * j + 1] = (i + 1, 1)
    singles = [(0, 0), (LMAX, 0)]
    for i in range(whole - left, whole):
        singles += [(i + 1, 0), (i + 1, 1)]
    for d, (m, p) in enumerate(singles):
        orders[d, pairs] = m
        units[d * rows + rows - 2] = (m, p)
    return rows, orders, units


def fourier_np(total, units, lon_count, lon_padded):
    forward = np.zeros((total, lon_padded))
    inverse = np.zeros((total, lon_padded))
    k = np.arange(lon_count)
    for at, (m, p) in units.items():
        angle = 2.0 * math.pi / lon_count * ((k * m) % lon_count)
        wave = np.cos(angle) if p == 0 else -np.sin(angle)
        doubling = 1.0 if m == 0 or 2 * m == lon_count else 2.0
        forward[at, :lon_count] = wave * (2.0 * math.pi / lon_count)
        inverse[at, :lon_count] = wave * doubling
    return forward.astype(np.float32), inverse.astype(np.float32)


def split_np(table):
    high = table.astype(ml_dtypes.bfloat16)
    low = (table - high.astype(np.float32)).astype(ml_dtypes.bfloat16)
    return jnp.asarray(high), jnp.asarray(low)


def split_x(table):
    high = lax.reduce_precision(table, 8, 7)
    return high.astype(BF16), (table - high).astype(BF16)


def split(value):
    high = value.astype(BF16)
    return high, (value - high.astype(F32)).astype(BF16)


def dot3(a, b):
    (ah, al), (bh, bl) = a, b
    dot = functools.partial(jnp.dot, preferred_element_type=F32)
    return dot(ah, bh) + (dot(ah, bl) + dot(al, bh))


def triple(value):
    high, low = split(value)
    return jnp.concatenate([high, high, low], axis=1)


def dot_triple(value, w_ref):
    w = w_ref[...].reshape(3 * w_ref.shape[1], w_ref.shape[2])
    return jnp.dot(triple(value), w, preferred_element_type=F32)


def params():
    return pltpu.CompilerParams(
        dimension_semantics=("arbitrary",), vmem_limit_bytes=VMEM_LIMIT
    )


def whole(shape):
    return pl.BlockSpec(shape, lambda i: (0,) * len(shape))


def diagonal(shape):
    return lax.broadcasted_iota(jnp.int32, shape, 1) == lax.broadcasted_iota(
        jnp.int32, shape, 2
    )


def analysis_body(shape, x, th_ref, tl_ref, o_ref):
    devices, rows, main = shape
    out = dot3((th_ref[...], tl_ref[...]), split(x))
    o_ref[...] = out[:, :main].reshape(devices, 1, rows, main)
    column = out[:, main : main + 1].reshape(devices, rows, 1)
    spare = jnp.where(diagonal((devices, rows, LANES)), column, 0.0).sum(axis=1)
    for d in range(devices):
        o_ref[d, 0, rows - 1 : rows, :LANES] = spare[d : d + 1, :]


def analysis_kernel(shape, x_ref, *refs):
    analysis_body(shape, x_ref[0], *refs)


def first_kernel(shape, part, state_ref, noise_ref, *refs):
    *tables, x_ref, o_ref, joined = refs
    lon, channels = state_ref.shape[1], state_ref.shape[3]
    base = channels // LANES * LANES

    @pl.when(pl.program_id(0) == 0)
    def _():
        joined[...] = jnp.zeros_like(joined)

    joined[:lon, :channels] = state_ref[0, :, part, :]
    lane = lax.broadcasted_iota(jnp.int32, noise_ref.shape[2:], 1)
    joined[:, base:] = jnp.where(lane < channels - base, joined[:, base:], noise_ref[0, 0])
    x = joined[...]
    x_ref[0] = x[:, : x_ref.shape[2]]
    analysis_body(shape, x, *tables, o_ref)


def analysis(x, first, row_count, table, plan, part=None):
    devices, rows, main = plan
    total, lon = table.shape
    th, tl = split_np(table)
    out_specs = [pl.BlockSpec((devices, 1, rows, main), lambda r: (0, r, 0, 0))]
    out_shape = [jax.ShapeDtypeStruct((devices, row_count, rows, main), F32)]
    scratch = []
    if part is None:
        kernel = functools.partial(analysis_kernel, plan)
        operands = [x]
        x_specs = [pl.BlockSpec((1, lon, main + 1), lambda r: (first + r, 0, 0))]
    else:
        kernel = functools.partial(first_kernel, plan, part)
        state, noise = operands = x
        x_specs = [
            pl.BlockSpec((1, *state.shape[1:]), lambda r: (r, 0, 0, 0)),
            pl.BlockSpec((1, 1, *noise.shape[2:]), lambda r: (part, r, 0, 0)),
        ]
        out_specs.insert(0, pl.BlockSpec((1, lon, main + 1), lambda r: (r, 0, 0)))
        out_shape.insert(0, jax.ShapeDtypeStruct((row_count, lon, main + 1), F32))
        scratch.append(pltpu.VMEM((lon, main + LANES), F32))
    return pl.pallas_call(
        kernel,
        grid=(row_count,),
        in_specs=x_specs + [whole((total, lon))] * 2,
        out_specs=out_specs,
        out_shape=out_shape,
        scratch_shapes=scratch,
        compiler_params=params(),
        cost_estimate=cost(1.2 * row_count),
        name="analysis",
    )(*operands, th, tl)


def synthesis_kernel(shape, joint, y_ref, th_ref, tl_ref, x_ref, *refs):
    devices, rows, main = shape
    *others, o_ref = refs
    total = devices * rows
    table = (th_ref[...], tl_ref[...])
    out = x_ref[0, :, :main] + dot3(table, split(y_ref[...].reshape(total, main)))
    if joint:
        lon, channels = o_ref.shape[1], o_ref.shape[3]
        for i, other in enumerate(others):
            o_ref[0, :, i, :] = other[0, :lon, :channels]
        o_ref[0, :, len(others), :] = out[:lon, :channels]
        return
    o_ref[0, :, :main] = out
    spare = y_ref[:, 0, rows - 1 : rows, :LANES]
    column = jnp.where(
        diagonal((devices, rows, LANES)), jnp.broadcast_to(spare, (devices, rows, LANES)), 0.0
    ).sum(axis=2, keepdims=True)
    column = jnp.broadcast_to(column.reshape(total, 1), (total, LANES))
    o_ref[0, :, main:] = x_ref[0, :, main:] + dot3(table, split(column))[:, :1]


def synthesis(y, table, x, first, held=None, joint=None):
    devices, row_count, rows, main = y.shape
    all_rows, lon, width = x.shape
    total = table.shape[0]
    th, tl = split_np(table.T.copy())
    x_spec = pl.BlockSpec((1, lon, width), lambda r: (first + r, 0, 0))
    operands = [y, th, tl, x]
    in_specs = [
        pl.BlockSpec((devices, 1, rows, main), lambda r: (0, r, 0, 0)),
        whole((lon, total)),
        whole((lon, total)),
        x_spec,
    ]
    out_spec, out_shape = x_spec, (all_rows, lon, width)
    aliases = {}
    if joint is not None:
        others, lon_out, channels = joint
        operands += others
        in_specs += [x_spec] * len(others)
        out_shape = (all_rows, lon_out, len(others) + 1, channels)
        out_spec = pl.BlockSpec((1, *out_shape[1:]), lambda r: (r, 0, 0, 0))
    elif held is not None:
        aliases = {len(operands): 0}
        operands.append(held)
        in_specs.append(pl.BlockSpec(memory_space=pl.ANY))
    return pl.pallas_call(
        functools.partial(synthesis_kernel, (devices, rows, main), joint is not None),
        grid=(row_count,),
        in_specs=in_specs,
        out_specs=out_spec,
        out_shape=jax.ShapeDtypeStruct(out_shape, F32),
        input_output_aliases=aliases,
        compiler_params=params(),
        cost_estimate=cost(1.2 * row_count),
        name="synthesis",
    )(*operands)


def halves(chains, rows):
    steps = len(chains[0][3])
    sizes = [rows >> k for k in range(steps + 1)]
    sides, starts = [], []
    for *_, order in chains:
        side, at = [], [0]
        for k, (axis, bit_at) in enumerate(order):
            me = lax.axis_index(axis)
            bit = (me // (1 << bit_at)) % 2
            side.append((bit, {axis: me + (1 - 2 * bit) * (1 << bit_at)}))
            at.append(at[-1] + bit * sizes[k + 1])
        sides.append(side)
        starts.append(at)
    return sides, starts, sizes


def greet(partners):
    barrier = pltpu.get_barrier_semaphore()
    for _, partner in partners:
        pl.semaphore_signal(
            barrier, inc=1, device_id=partner, device_id_type=pl.DeviceIdType.MESH
        )
    pl.semaphore_wait(barrier, len(partners))


def send_to(partner, source, target, send, recv):
    return pltpu.make_async_remote_copy(
        src_ref=source,
        dst_ref=target,
        send_sem=send,
        recv_sem=recv,
        device_id=partner,
        device_id_type=pl.DeviceIdType.MESH,
    )


def scatter_sum_kernel(chains, near, arrays, *refs):
    count, steps = len(chains), len(chains[0][3])
    ins, outs, refs = refs[:arrays], refs[arrays : 2 * arrays], refs[2 * arrays :]
    send, recv = refs[-2:]
    kept, landed = refs[:count], refs[count:-2]
    sides, starts, sizes = halves(chains, ins[0].shape[0])
    lanes = [pl.ds(first, size) for _, first, size, _ in chains]
    greet(sides[0])

    def halve(c, k):
        bit, partner = sides[c][k]
        give = starts[c][k] + (1 - bit) * sizes[k + 1]
        give = pl.ds(pl.multiple_of(give, 8), sizes[k + 1])
        source = ins[chains[c][0]].at[give, lanes[c]] if k == 0 else kept[c].at[give]
        return send_to(partner, source, landed[c * steps + k], send.at[c, k], recv.at[c, k])

    def share(c, k):
        return pl.ds(pl.multiple_of(starts[c][k] - starts[c][near], 8), sizes[k])

    def double(c, k):
        have = outs[chains[c][0]].at[share(c, k + 1), lanes[c]]
        step = 2 * steps - 1 - k
        return send_to(sides[c][k][1], have, have, send.at[c, step], recv.at[c, step])

    flying = []
    for c in range(count):
        flying.append(halve(c, 0))
        flying[c].start()
    for k in range(steps):
        for c in range(count):
            flying[c].wait()
            rows = pl.ds(pl.multiple_of(starts[c][k + 1], 8), sizes[k + 1])
            mine = ins[chains[c][0]][rows, lanes[c]] if k == 0 else kept[c][rows, :]
            total = mine + landed[c * steps + k][...]
            if k + 1 < steps:
                kept[c][rows, :] = total
                flying[c] = halve(c, k + 1)
            else:
                outs[chains[c][0]][share(c, steps), lanes[c]] = total
                flying[c] = double(c, k)
            flying[c].start()
    for k in reversed(range(near, steps)):
        for c in range(count):
            flying[c].wait()
            if k > near:
                flying[c] = double(c, k - 1)
                flying[c].start()


def gather_kernel(chains, near, arrays, *refs):
    count = len(chains)
    ins, outs, (send, recv) = refs[:arrays], refs[arrays : 2 * arrays], refs[2 * arrays :]
    sides, starts, sizes = halves(chains, outs[0].shape[0])
    lanes = [pl.ds(first, size) for _, first, size, _ in chains]
    greet(sides[0][:near])

    def double(c, k):
        rows = pl.ds(pl.multiple_of(starts[c][k + 1], 8), sizes[k + 1])
        have = outs[chains[c][0]].at[rows, lanes[c]]
        return send_to(sides[c][k][1], have, have, send.at[c, k], recv.at[c, k])

    flying = []
    for c in range(count):
        rows = pl.ds(pl.multiple_of(starts[c][near], 8), sizes[near])
        outs[chains[c][0]][rows, lanes[c]] = ins[chains[c][0]][:, lanes[c]]
        flying.append(double(c, near - 1))
        flying[c].start()
    for k in reversed(range(near)):
        for c in range(count):
            flying[c].wait()
            if k > 0:
                flying[c] = double(c, k - 1)
                flying[c].start()


def lane_chains(arrays, width, orders):
    cut = width // (2 * LANES) * LANES
    both = ((0, cut, orders[0]), (cut, width - cut, orders[1]))
    return [(i, *half) for i in range(arrays) for half in both]


def remote_params(collective_id):
    return pltpu.CompilerParams(
        collective_id=collective_id, has_side_effects=True, vmem_limit_bytes=VMEM_LIMIT
    )


def scatter_sum(xs, orders, near, collective_id):
    rows, width = xs[0].shape
    steps = len(orders[0])
    chains = lane_chains(len(xs), width, orders)
    vmem = pl.BlockSpec(memory_space=pltpu.VMEM)
    return pl.pallas_call(
        functools.partial(scatter_sum_kernel, chains, near, len(xs)),
        in_specs=[vmem] * len(xs),
        out_specs=[vmem] * len(xs),
        out_shape=[jax.ShapeDtypeStruct((rows >> near, width), F32)] * len(xs),
        scratch_shapes=[pltpu.VMEM((rows, size), F32) for _, _, size, _ in chains]
        + [
            pltpu.VMEM((rows >> (k + 1), size), F32)
            for _, _, size, _ in chains
            for k in range(steps)
        ]
        + [pltpu.SemaphoreType.DMA((len(chains), 2 * steps))] * 2,
        compiler_params=remote_params(collective_id),
        cost_estimate=cost(80),
        name="scatter_sum",
    )(*xs)


def gather(xs, orders, near, collective_id):
    rows, width = xs[0].shape
    chains = lane_chains(len(xs), width, orders)
    vmem = pl.BlockSpec(memory_space=pltpu.VMEM)
    return pl.pallas_call(
        functools.partial(gather_kernel, chains, near, len(xs)),
        in_specs=[vmem] * len(xs),
        out_specs=[vmem] * len(xs),
        out_shape=[jax.ShapeDtypeStruct((rows << near, width), F32)] * len(xs),
        scratch_shapes=[pltpu.SemaphoreType.DMA((len(chains), near))] * 2,
        compiler_params=remote_params(collective_id),
        cost_estimate=cost(40),
        name="gather",
    )(*xs)


def weights_kernel(hidden, main, a_ref, b_ref, *refs):
    for w_ref, (plain, flipped, e) in zip((a_ref, b_ref), (refs[:3], refs[3:])):
        w = w_ref[...]
        column = lax.broadcasted_iota(jnp.int32, w.shape, 1) + pl.program_id(0) * LANES
        w = jnp.where(column < hidden, w, 0.0)
        for ref, value in ((plain, w[:main]), (flipped, w[:main].T)):
            high, low = split(value)
            ref[0] = high
            ref[1] = low
            ref[2] = high
        e[...] = w[main : main + 1]


def prepare_weights(a, b):
    width, hidden = a.shape
    main = width // LANES * LANES
    tiles = (hidden + LANES - 1) // LANES
    across = pl.BlockSpec((3, main, LANES), lambda i: (0, 0, i))
    down = pl.BlockSpec((3, LANES, main), lambda i: (0, i, 0))
    row = pl.BlockSpec((1, LANES), lambda i: (0, i))
    total = tiles * LANES
    shapes = [
        jax.ShapeDtypeStruct((3, main, total), BF16),
        jax.ShapeDtypeStruct((3, total, main), BF16),
        jax.ShapeDtypeStruct((1, total), F32),
    ]
    out = pl.pallas_call(
        functools.partial(weights_kernel, hidden, main),
        grid=(tiles,),
        in_specs=[pl.BlockSpec((width, LANES), lambda i: (0, i))] * 2,
        out_specs=[across, down, row] * 2,
        out_shape=shapes * 2,
        compiler_params=params(),
        cost_estimate=cost(12),
        name="weights",
    )(a, b)
    return out[:3], out[3:]


def lane_mask(shape, j):
    lane = lax.broadcasted_iota(jnp.int32, shape, 1)
    return (lane == 2 * j) | (lane == 2 * j + 1)


def filter_kernel(shape, backward, *refs):
    in_sizes, out_sizes, rows = shape
    g_refs, refs = refs[: len(in_sizes)], refs[len(in_sizes) :]
    ah_ref, al_ref, bh_ref, bl_ref, gain_ref, egain_ref = refs[:6]
    refs = refs[6:]
    if backward:
        c_ref, ec_ref = refs[:2]
        refs = refs[2:]
    h_refs, refs = refs[: len(out_sizes)], refs[len(out_sizes) :]
    if backward:
        gg_ref, egg_ref = refs
    else:
        c_ref, ec_ref = refs
    tables = rows // 2
    slots = sum(out_sizes)

    def load(u):
        parts = [
            ref[pl.ds(u, n, stride=rows), :] for ref, n in zip(g_refs, in_sizes)
        ]
        return parts[0] if len(parts) == 1 else jnp.concatenate(parts, axis=0)

    def store(u, value):
        first = 0
        for ref, n in zip(h_refs, out_sizes):
            ref[pl.ds(u, n, stride=rows), :] = value[first : first + n, :]
            first += n

    gain = gain_ref[...]
    gain2 = jnp.concatenate([gain, gain], axis=1)
    total = jnp.zeros(gain.shape, F32)
    for j in range(tables):
        x = jnp.concatenate([load(2 * j), load(2 * j + 1)], axis=1)
        c = dot3((ah_ref[j], al_ref[j]), split(x))
        if backward:
            total += c_ref[2 * j] * c[:, :LANES]
            if j < tables - 1:
                total += c_ref[2 * j + 1] * c[:, LANES:]
        else:
            c_ref[2 * j] = c[:, :LANES]
            c_ref[2 * j + 1] = c[:, LANES:]
        y = dot3((bh_ref[j], bl_ref[j]), split(c * gain2))
        store(2 * j, y[:, :LANES])
        store(2 * j + 1, y[:, LANES:])
    if backward:
        gg_ref[...] = total

    @pl.when(pl.program_id(0) == 0)
    def _():
        x = split(load(rows - 1))
        c = jnp.zeros(gain.shape, F32)
        for j in range(tables):
            mine = dot3((ah_ref[j], al_ref[j]), x)
            c = jnp.where(lane_mask(c.shape, j), mine, c)
        if backward:
            egg_ref[...] = ec_ref[...] * c
        else:
            ec_ref[...] = c
        c = split(c * egain_ref[...])
        y = jnp.zeros((slots, LANES), F32)
        for j in range(tables):
            mine = dot3((bh_ref[j], bl_ref[j]), c)
            y = jnp.where(lane_mask(y.shape, j), mine, y)
        store(rows - 1, y)


def filter_slots(gs, first, second, gain, out_rows, coeffs=None):
    devices, _, rows, main = gs[0].shape
    in_sizes = [devices * g.shape[1] for g in gs]
    out_sizes = [devices * n for n in out_rows]
    slots = sum(in_sizes)
    degrees = first[0].shape[1]
    backward = coeffs is not None
    block = lambda n: pl.BlockSpec((n * rows, LANES), lambda t: (0, t))
    c_spec = pl.BlockSpec((rows, degrees, LANES), lambda t: (0, 0, t))
    ec_spec = whole((degrees, LANES))
    gg_spec = pl.BlockSpec((degrees, LANES), lambda t: (0, t))
    main_gain, extra_gain = gain
    in_specs = [block(n) for n in in_sizes] + [
        whole(first[0].shape),
        whole(first[0].shape),
        whole(second[0].shape),
        whole(second[0].shape),
        gg_spec,
        whole((degrees, 1)),
    ]
    operands = [g.reshape(-1, main) for g in gs]
    operands += [*first, *second, main_gain, extra_gain]
    out_shape = [jax.ShapeDtypeStruct((n * rows, main), F32) for n in out_sizes]
    out_specs = [block(n) for n in out_sizes]
    if backward:
        in_specs += [c_spec, ec_spec]
        operands += list(coeffs)
        out_shape.append(jax.ShapeDtypeStruct((degrees, main), F32))
        out_specs.append(gg_spec)
    else:
        out_shape.append(jax.ShapeDtypeStruct((rows, degrees, main), F32))
        out_specs.append(c_spec)
    out_shape.append(jax.ShapeDtypeStruct((degrees, LANES), F32))
    out_specs.append(ec_spec)
    *h, c, ec = pl.pallas_call(
        functools.partial(filter_kernel, (in_sizes, out_sizes, rows), backward),
        grid=(main // LANES,),
        in_specs=in_specs,
        out_specs=out_specs,
        out_shape=out_shape,
        compiler_params=params(),
        cost_estimate=cost(12),
        name="filter_back" if backward else "filter",
    )(*operands)
    h = [x.reshape(devices, n, rows, main) for x, n in zip(h, out_rows)]
    return h, (c, ec)


def mlp_kernel(main, m_ref, w1, w1e, b1, w2, w2e, b2, b2e, *refs):
    act_ref, slope_ref, out_ref, field_ref = refs[-4:]
    m = m_ref[:, :main]
    extra = m_ref[:, main:]
    v = dot_triple(m, w1) + extra * w1e[...] + b1[...]
    cdf = 0.5 * (1.0 + lax.erf(v * (1.0 / math.sqrt(2.0))))
    slope_ref[...] = cdf + v * jnp.exp(-0.5 * v * v) * (1.0 / math.sqrt(2.0 * math.pi))
    act = v * cdf
    act_ref[...] = act
    out = m + dot_triple(act, w2) + b2[...]
    out_ref[:, :main] = out
    field_ref[...] = out
    last = jnp.sum(act * w2e[...], axis=1, keepdims=True)
    out_ref[:, main:] = extra + last + b2e[...]


def tile_of(tokens, most):
    tile = most // 8 * 8
    while tokens % tile:
        tile -= 8
    return tile


def mlp(mixed, first, tokens, weights, held):
    whole_count, width = mixed.shape
    w1, w1e, b1, w2, w2e, b2, b2e = weights
    _, main, hidden = w1.shape
    tile = tile_of(math.gcd(first, tokens), 368)
    at = first // tile
    row = lambda n: pl.BlockSpec((tile, n), lambda i: (at + i, 0))
    shape = lambda n: jax.ShapeDtypeStruct((whole_count, n), F32)
    operands = [mixed, w1, w1e, b1, w2, w2e, b2, b2e]
    in_specs = [row(width)] + [whole(x.shape) for x in operands[1:]]
    aliases = {len(operands) + i: i for i in range(len(held))}
    return pl.pallas_call(
        functools.partial(mlp_kernel, main),
        grid=(tokens // tile,),
        in_specs=in_specs + [pl.BlockSpec(memory_space=pl.ANY)] * len(held),
        out_specs=(
            row(hidden),
            row(hidden),
            row(width),
            pl.BlockSpec((tile, main), lambda i: (i, 0)),
        ),
        out_shape=(
            shape(hidden),
            shape(hidden),
            shape(width),
            jax.ShapeDtypeStruct((tokens, main), F32),
        ),
        input_output_aliases=aliases,
        compiler_params=params(),
        cost_estimate=cost(0.023 * tokens),
        name="mlp",
    )(*operands, *held)


def mlp_back_kernel(main, g_ref, slope_ref, w2, w1, w1e, *refs):
    pre_ref, gm_ref, bias_in_ref, bias_out_ref = refs[-4:]

    @pl.when(pl.program_id(0) == 0)
    def _():
        bias_in_ref[...] = jnp.zeros_like(bias_in_ref)
        bias_out_ref[...] = jnp.zeros_like(bias_out_ref)

    g = g_ref[...]
    pre = dot_triple(g, w2) * slope_ref[...]
    pre_ref[...] = pre
    gm_ref[:, :main] = g + dot_triple(pre, w1)
    gm_ref[:, main:] = jnp.sum(pre * w1e[...], axis=1, keepdims=True)
    bias_in_ref[...] += jnp.sum(pre, axis=0, keepdims=True)
    bias_out_ref[...] += jnp.sum(g, axis=0, keepdims=True)


def mlp_back(g, slope, first, weights, held):
    tokens, main = g.shape
    whole_count, hidden = slope.shape
    w2, w1, w1e = weights
    tile = tile_of(math.gcd(first, tokens), 368)
    at = first // tile
    row = lambda n: pl.BlockSpec((tile, n), lambda i: (at + i, 0))
    shape = lambda n: jax.ShapeDtypeStruct((whole_count, n), F32)
    operands = [g, slope, w2, w1, w1e]
    in_specs = [pl.BlockSpec((tile, main), lambda i: (i, 0)), row(hidden)]
    in_specs += [whole(x.shape) for x in operands[2:]]
    aliases = {len(operands) + i: i for i in range(len(held))}
    return pl.pallas_call(
        functools.partial(mlp_back_kernel, main),
        grid=(tokens // tile,),
        in_specs=in_specs + [pl.BlockSpec(memory_space=pl.ANY)] * len(held),
        out_specs=(row(hidden), row(main + 1), whole((1, hidden)), whole((1, main))),
        out_shape=(
            shape(hidden),
            shape(main + 1),
            jax.ShapeDtypeStruct((1, hidden), F32),
            jax.ShapeDtypeStruct((1, main), F32),
        ),
        input_output_aliases=aliases,
        compiler_params=params(),
        cost_estimate=cost(0.021 * tokens),
        name="mlp_back",
    )(*operands, *held)


def crps_kernel(shape, groups_ref, *refs):
    own, sources, lane_tiles, channels = shape
    members = own * sources
    f_refs = refs[:members]
    t_ref, a_ref = refs[members : members + 2]
    g_refs = refs[members + 2 : 2 * members + 2]
    loss_ref, f_all, g_all = refs[2 * members + 2 :]
    pair_scale = 1.0 / (ENSEMBLE_SIZE * (ENSEMBLE_SIZE - 1))

    @pl.when(pl.program_id(0) == 0)
    def _():
        loss_ref[...] = jnp.zeros_like(loss_ref)

    def chunk(i, total):
        rows = pl.ds(pl.multiple_of(i * 8, 8), 8)
        area = jnp.broadcast_to(a_ref[rows, :], (8, LANES))
        for j in range(lane_tiles):
            lanes = slice(j * LANES, (j + 1) * LANES)
            weight = area
            if (j + 1) * LANES > channels:
                lane = lax.broadcasted_iota(jnp.int32, area.shape, 1)
                weight = jnp.where(lane + j * LANES < channels, area, 0.0)
            for source in range(sources):
                for b in range(own):
                    f_all[source * own + b] = f_refs[source * own + b][rows, lanes]
            for d in range(DATES):
                places = [groups_ref[d * ENSEMBLE_SIZE + i] for i in range(ENSEMBLE_SIZE)]
                f = [f_all[m] for m in places]
                observed = t_ref[d, rows, lanes]
                skill = jnp.zeros_like(area)
                couple = jnp.zeros_like(area)
                grads = []
                for v in f:
                    v = v - observed
                    square = v * v + 1.0
                    inverse = lax.rsqrt(square)
                    skill += square * inverse
                    grads.append(v * inverse * (1.0 / ENSEMBLE_SIZE))
                for m in range(ENSEMBLE_SIZE):
                    for n in range(m + 1, ENSEMBLE_SIZE):
                        v = f[m] - f[n]
                        square = v * v + 1.0
                        inverse = lax.rsqrt(square)
                        couple += square * inverse
                        v = v * inverse * pair_scale
                        grads[m] -= v
                        grads[n] += v
                total += weight * (skill * (1.0 / ENSEMBLE_SIZE) - couple * pair_scale)
                for m, grad in zip(places, grads):
                    g_all[m] = weight * grad
            for source in range(sources):
                for b in range(own):
                    g_refs[source * own + b][rows, lanes] = g_all[source * own + b]
        return total

    count = a_ref.shape[0] // 8
    loss_ref[...] += lax.fori_loop(0, count, chunk, jnp.zeros((8, LANES), F32))


def crps(fields, own, observed, area, places, channels):
    members = len(fields)
    points, main = fields[0].shape
    tile = points // 2 if points % 16 == 0 else points
    spec = pl.BlockSpec((tile, main), lambda i, g: (i, 0))
    *grads, loss = pl.pallas_call(
        functools.partial(crps_kernel, (own, members // own, main // LANES, channels)),
        grid_spec=pltpu.PrefetchScalarGridSpec(
            num_scalar_prefetch=1,
            grid=(points // tile,),
            in_specs=[spec] * members
            + [
                pl.BlockSpec((DATES, tile, main), lambda i, g: (0, i, 0)),
                pl.BlockSpec((tile, 1), lambda i, g: (i, 0)),
            ],
            out_specs=[spec] * members + [pl.BlockSpec((8, LANES), lambda i, g: (0, 0))],
            scratch_shapes=[pltpu.VMEM((members, 8, LANES), F32)] * 2,
        ),
        out_shape=[jax.ShapeDtypeStruct((points, main), F32)] * members
        + [jax.ShapeDtypeStruct((8, LANES), F32)],
        compiler_params=params(),
        cost_estimate=cost(0.045 * points),
        name="crps",
    )(places, *fields, observed, area)
    return grads, jnp.sum(loss)


def local(
    state_now,
    sample_random_maps,
    noise_scale,
    spec_gain,
    weight_in,
    bias_in,
    weight_out,
    bias_out,
    targets,
    date_of,
    row_slot,
):
    highest, high = lax.Precision.HIGHEST, lax.Precision.HIGH
    own, row_count, lon, channels = state_now.shape
    width, hidden = weight_in.shape
    main = width // LANES * LANES
    devices = lax.axis_size("lat")
    sources = lax.axis_size("member")
    lat_rank = lax.axis_index("lat")
    member_rank = lax.axis_index("member")
    slots = devices * row_count
    members = own * sources

    groups = [row_count // 3] * 3 if row_count % 3 == 0 else [row_count]
    starts = [sum(groups[:q]) for q in range(len(groups))]
    padded = (lon + 7) // 8 * 8
    while any(n * padded % (8 * sources) for n in groups):
        padded += 8
    points = [n * padded // sources for n in groups]

    rows, orders, units = unit_plan(devices)
    plan = (devices, rows, main)
    forward_table, inverse_table = fourier_np(devices * rows, units, lon, padded)
    degrees = (LMAX + 8) // 8 * 8
    full = np.zeros((LMAX + 1, degrees, NLAT), np.float32)
    full[:, : LMAX + 1] = legendre_np().astype(np.float32)
    mine = lax.dynamic_index_in_dim(jnp.asarray(full[orders]), lat_rank, 0, keepdims=False)
    sine = np.sin((np.arange(NLAT) + 0.5) * (math.pi / NLAT))
    geometry = jnp.asarray(
        np.stack(
            [np.ones(NLAT), math.pi / NLAT * sine, NLAT * sine / np.sum(sine)]
        ).astype(np.float32)
    )

    def low_tables(blocks):
        ids = np.arange(slots, dtype=np.int32).reshape(devices, row_count)
        ids = np.concatenate([ids[:, a : a + n].reshape(-1) for a, n in blocks])
        hits = (row_slot[:, None] == jnp.asarray(ids)[None, :]).astype(F32)
        quadrature = jnp.dot(geometry, hits, precision=highest)[1]
        table = jnp.einsum("jla,as->jls", mine, hits, precision=highest)
        weighted, plain = split_x(table * quadrature), split_x(table)
        flip = lambda pair: tuple(jnp.swapaxes(t, 1, 2) for t in pair)
        return weighted, plain, flip(weighted), flip(plain)

    in_full = low_tables([(0, row_count)])
    in_groups = low_tables(list(zip(starts, groups)))

    own_ids = lat_rank * row_count + jnp.arange(row_count, dtype=jnp.int32)
    hits_own = (row_slot[:, None] == own_ids[None, :]).astype(F32)
    used_own, _, area_own = jnp.dot(geometry, hits_own, precision=highest)
    gain = jnp.pad(spec_gain, ((0, degrees - LMAX - 1), (0, 0)))
    gain = (gain[:, :main], gain[:, main:])

    hidden_padded = (hidden + LANES - 1) // LANES * LANES
    pad_cols = lambda w: jnp.pad(w, ((0, 0), (0, hidden_padded - hidden)))
    w1_parts, w2t_parts = prepare_weights(weight_in, weight_out.T)
    forward_weights = (
        w1_parts[0],
        w1_parts[2],
        pad_cols(bias_in[None, :]),
        w2t_parts[1],
        w2t_parts[2],
        bias_out[None, :main],
        bias_out[None, main:],
    )
    backward_weights = (w2t_parts[0], w1_parts[1], w1_parts[2])

    base = channels // LANES * LANES
    noise = jnp.pad(
        noise_scale[:, None, None, :] * sample_random_maps,
        ((0, 0), (0, 0), (0, padded - lon), (channels - base, main + LANES - width)),
    )
    state = jnp.transpose(state_now, (1, 2, 0, 3))
    observed = jnp.pad(
        targets, ((0, 0), (0, 0), (0, padded - lon), (0, main - channels))
    )
    token_area = jnp.where(jnp.arange(padded)[None, :] < lon, area_own[:, None], 0.0)
    observed_share, area_share = [], []
    for a, n, size in zip(starts, groups, points):
        o = observed[:, a : a + n].reshape(DATES, n * padded, main)
        o = lax.dynamic_slice_in_dim(o, member_rank * size, size, axis=1)
        t = token_area[a : a + n].reshape(n * padded, 1)
        t = lax.dynamic_slice_in_dim(t, member_rank * size, size, axis=0)
        observed_share.append(o)
        area_share.append(t)
    by_date = jnp.argsort(date_of, stable=True).astype(jnp.int32)
    places = ((by_date // own) ^ member_rank) * own + by_date % own

    def tie(x, *tokens):
        return lax.optimization_barrier((x, tokens))[0]

    moved = []

    def to_owner(x):
        x = tie(x, *moved[-1:])
        moved.append(lax.all_to_all(x, "lat", split_axis=0, concat_axis=0, tiled=True))
        return moved[-1]

    def swap(x, distance):
        if distance == 0:
            return x
        pairs = [(i, i ^ distance) for i in range(sources)]
        return lax.ppermute(x, "member", pairs)

    def exchange(q, field):
        size = points[q]
        shares = []
        for distance in range(sources):
            share = lax.dynamic_slice_in_dim(
                field, (member_rank ^ distance) * size, size, axis=0
            )
            shares.append(swap(share, distance))
        return shares

    every = range(len(groups))
    final = own - 1

    inputs, spectra, synths, coeffs = [], [], [], []
    for b in range(own):
        if b > 0:
            state, noise = tie((state, noise), f)
        x, f = analysis((state, noise), 0, row_count, forward_table, plan, b)
        inputs.append(x)
        spectra.append(to_owner(f))
    prepared = (forward_weights, backward_weights, observed_share, area_share, places)
    for b in range(own):
        if b > 0:
            spectra[b] = tie(spectra[b], *h)
        if b == final:
            spectra[b], prepared = lax.optimization_barrier((spectra[b], prepared))
        h, c = filter_slots(
            [spectra[b]],
            in_full[0],
            in_groups[3] if b == final else in_full[3],
            gain,
            groups if b == final else [row_count],
        )
        coeffs.append(c)
        synths.append([to_owner(h[0])])
    forward_weights, backward_weights, observed_share, area_share, places = prepared

    mixed, held, shares = [None] * own, [[] for _ in range(own)], {}

    def mix(b, q, *tokens):
        first, y = (starts[q], synths[b][q]) if b == final else (0, synths[b][0])
        y = tie(y, *tokens)
        mixed[b] = synthesis(y, inverse_table, inputs[b], first, mixed[b])

    def forward(b, q, *tokens):
        m = tie(mixed[b], *tokens).reshape(row_count * padded, width)
        *held[b], field = mlp(
            m, starts[q] * padded, groups[q] * padded, forward_weights, held[b]
        )
        shares[b, q] = exchange(q, field)
        return field

    results, got = {}, {}
    losses = []

    def score(q, *tokens):
        fields = [shares[b, q][d] for d in range(sources) for b in range(own)]
        fields = tie(fields, *tokens)
        out, part = crps(fields, own, observed_share[q], area_share[q], places, channels)
        losses.append(part)
        results[q] = out
        if q != 1:
            got[0, q] = returned(0, q)
        return out[0]

    def returned(b, q):
        return [swap(results[q][d * own + b], d) for d in range(sources)]

    def gradient(b, parts):
        size = sum(groups[q] for q in parts) * padded
        g = jnp.zeros((size, main), F32)
        for q in parts:
            for distance, share in enumerate(got[b, q]):
                at = (member_rank ^ distance) * points[q]
                at += (starts[q] - starts[parts[0]]) * padded
                g = lax.dynamic_update_slice_in_dim(g, share, at, axis=0)
        return g

    grads = [[] for _ in range(own)]
    slopes, back_held = {}, [[] for _ in range(own)]
    bias_in_sums, bias_out_sums = [], []
    back = [[] for _ in range(own)]

    def backward(b, q, *tokens):
        g = tie(gradient(b, [q]), *tokens)
        *back_held[b], b1, b2 = mlp_back(
            g, held[b][1], starts[q] * padded, backward_weights, back_held[b]
        )
        grads[b].append(g)
        bias_in_sums.append(b1)
        bias_out_sums.append(b2)
        return b2

    def send_back(b, parts):
        gm = tie(back_held[b][1], *moved[-1:]) if b > 0 or parts[0] > 0 else back_held[b][1]
        gm = gm.reshape(row_count, padded, width)
        size = sum(groups[q] for q in parts)
        f = analysis(gm, starts[parts[0]], size, inverse_table, plan)[0]
        back[b].append(to_owner(f))
        return f

    token = ()
    for b in range(final):
        mix(b, 0, *token)
        for q in every:
            token = (forward(b, q, *token),)
            if b == final - 1 and q == 1:
                synths[final].append(to_owner(tie(h[1], *token)))
    ready = lambda q: [shares[b, q] for b in range(final)]
    if len(groups) == 3:
        for q in (0, 1):
            mix(final, q, ready(q), *token)
            token = (forward(final, q),)
            if q == 0:
                synths[final].append(to_owner(tie(h[2], *token)))
        token = (score(0, ready(2), *token),)
        token = (score(1, *token),)
        first_back = backward(0, 0, synths[final][2], *token)
        results[1] = tie(results[1], first_back)
        got[0, 1] = returned(0, 1)
        for b in range(1, own):
            results[0] = tie(results[0], got[0, 1])
            got[b, 0] = returned(b, 0)
        token = (send_back(0, [0]),)
        mix(final, 2, *token)
        token = (forward(final, 2),)
        backward(0, 1, *token)
        token = (send_back(0, [1]),)
        token = (score(2, *token),)
        for b in range(1, own):
            token = (backward(b, 0, *token),)
            results[1] = tie(results[1], got[0, 2])
            got[b, 1] = returned(b, 1)
            results[2] = tie(results[2], got[b, 1])
            got[b, 2] = returned(b, 2)
        backward(0, 2, *token)
        token = (send_back(0, [2]),)
        for b in range(1, own):
            token = (backward(b, 1, *token),)
            token = (backward(b, 2, *token),)
            token = (send_back(b, list(every)),)
    else:
        for q in every:
            mix(final, q, *token)
            token = (forward(final, q),)
        for q in every:
            token = (score(q, *token),)
        for b in range(own):
            for q in every:
                if b > 0 or q == 1:
                    got[b, q] = returned(b, q)
                token = (backward(b, q, *token),)
            token = (send_back(b, list(every)),)
    loss = sum(losses)
    mixed = [m.reshape(row_count * padded, width) for m in mixed]
    act = [h[0] for h in held]
    block = [h[2] for h in held]
    g_pre = [h[0] for h in back_held]
    g_mixed = [h[1] for h in back_held]

    grads = tie(grads, *token)
    grad_out_t = 0.0
    for b in range(own):
        at = 0
        for g in grads[b]:
            n = g.shape[0]
            grad_out_t += jnp.einsum("tc,th->ch", g, act[b][at : at + n], precision=high)
            at += n
    g_pre = tie(g_pre, *token)
    grad_in = sum(
        jnp.einsum("tc,th->ch", mixed[b], g_pre[b], precision=high) for b in range(own)
    )
    grad_bias_in = sum(bias_in_sums)[0, :hidden]
    grad_bias_out = jnp.pad(sum(bias_out_sums)[0], (0, width - main))

    back[0], grad_out_t, grad_in = lax.optimization_barrier((back[0], grad_out_t, grad_in))
    spreads = []
    gain_by_member = []
    for b in range(own):
        split_in = len(back[b]) > 1
        (h,), (gg, egg) = filter_slots(
            back[b],
            in_groups[1] if split_in else in_full[1],
            in_full[2],
            gain,
            [row_count],
            coeffs[b],
        )
        if b == final:
            last_filtered = h
        else:
            spreads.append(to_owner(h))
        low = jnp.concatenate([gg, jnp.sum(egg, axis=1, keepdims=True)], axis=1)
        gain_by_member.append(low[: LMAX + 1])
    grad_gain = sum(gain_by_member)

    scale_parts = []
    for b in range(own):
        gm = g_mixed[b].reshape(row_count, padded, width)[:, :lon, channels:]
        direct = jnp.sum(gm * sample_random_maps[b], axis=(0, 1))
        spectral = jnp.sum(
            spec_gain[:, channels:] * gain_by_member[b][:, channels:], axis=0
        )
        scale_parts.append(direct + spectral / noise_scale[b])
    noise_count = width - channels
    scale_row = lax.dynamic_update_slice(
        jnp.zeros((members * noise_count,), F32),
        jnp.concatenate(scale_parts),
        (member_rank * own * noise_count,),
    )
    line = lambda v: jnp.pad(v, (0, -v.shape[0] % width)).reshape(-1, width)
    small = [grad_bias_out, grad_bias_in, jnp.concatenate([loss[None], scale_row])]
    small = [line(v) for v in small]
    pack = jnp.concatenate([grad_gain] + small, axis=0)
    bits = [("lat", 0), ("member", 0), ("member", 1)]
    bits += [("lat", k) for k in range(1, devices.bit_length() - 1)]
    if sources == 4 and len(bits) <= 5:
        lanes = hidden_padded
        flat = pack.reshape(-1)
        flat = jnp.pad(flat, (0, -flat.shape[0] % lanes)).reshape(-1, lanes)
        unit = 8 << len(bits)
        size = -(-(width + flat.shape[0]) // unit) * unit
        first = jnp.concatenate([grad_in, flat])
        arrays = [jnp.pad(x, ((0, size - x.shape[0]), (0, 0))) for x in (first, grad_out_t)]
        orders = [bits, [bits[0], bits[2], bits[1]] + bits[3:]]
        arrays = scatter_sum(tie(arrays, last_filtered), orders, 3, 1)
        last_filtered, arrays = lax.optimization_barrier((last_filtered, arrays))
        arrays = gather(tie(arrays, *spreads), orders, 3, 2)
        block, (first, second) = lax.optimization_barrier((block, arrays))
        grad_in, grad_out_t = first[:width, :hidden], second[:main, :hidden]
        flat = first[width : width + flat.shape[0]].reshape(-1)
        pack = flat[: pack.size].reshape(pack.shape)
    else:
        grad_in, grad_out_t, pack = lax.psum(
            (grad_in[:, :hidden], grad_out_t[:, :hidden], pack), ("member", "lat")
        )
    layer_output = jnp.stack(
        [x.reshape(row_count, padded, width)[:, :lon] for x in block]
    ) * used_own[None, :, None, None]
    done = []
    spreads.append(to_owner(last_filtered))
    for b in range(own):
        done.append(
            synthesis(
                tie(spreads[b], *done),
                forward_table,
                g_mixed[b].reshape(row_count, padded, width),
                0,
                joint=(done, lon, channels) if b == final else None,
            )
        )
    grad_state = jnp.transpose(done[-1], (2, 0, 1, 3))
    at = LMAX + 1
    grad_gain = pack[:at]
    grad_bias_out = pack[at]
    after = at + 1 + small[1].shape[0]
    grad_bias_in = pack[at + 1 : after].reshape(-1)[:hidden]
    last_row = pack[after:].reshape(-1)
    crps_loss = last_row[0] / (DATES * NLAT * NLON * channels)
    grad_scale = lax.dynamic_slice_in_dim(
        last_row, 1 + member_rank * own * noise_count, own * noise_count
    ).reshape(own, noise_count)
    grad_weight_out = jnp.pad(grad_out_t, ((0, width - main), (0, 0))).T

    return (
        crps_loss,
        layer_output,
        grad_state,
        grad_scale,
        grad_gain,
        grad_in,
        grad_bias_in,
        grad_weight_out,
        grad_bias_out,
    )


def solution(mesh):
    return jax.shard_map(
        local,
        mesh=mesh,
        in_specs=(
            P("member", "lat", None, None),
            P("member", "lat", None, None),
            P("member", None),
            P(),
            P(),
            P(),
            P(),
            P(),
            P(None, "lat", None, None),
            P(),
            P(),
        ),
        out_specs=(
            P(),
            P("member", "lat", None, None),
            P("member", "lat", None, None),
            P("member", None),
            P(),
            P(),
            P(),
            P(),
            P(),
        ),
        check_vma=False,
    )
```

```python
import functools
import math

import jax
import jax.numpy as jnp
import ml_dtypes
import numpy as np
from jax import lax
from jax.experimental import pallas as pl
from jax.experimental.pallas import tpu as pltpu
from jax.sharding import PartitionSpec as P

VARIABLE_COUNT = 633
LMAX = 90
NLAT = 90
NLON = 180
ENSEMBLE_SIZE = 4
DATES = 2

LANES = 128
VMEM_LIMIT = 56 * 1024 * 1024
F32 = jnp.float32
BF16 = jnp.bfloat16


def cost(microseconds):
    return pl.CostEstimate(
        flops=int(microseconds * 1.0e9), bytes_accessed=1000, transcendentals=0
    )


def legendre_np():
    colat = (np.arange(NLAT) + 0.5) * (math.pi / NLAT)
    cosine, log_sine = np.cos(colat), np.log(np.sin(colat))
    table = np.zeros((LMAX + 1, LMAX + 1, NLAT))
    for m in range(LMAX + 1):
        start = 0.5 * (
            math.log(2.0 * m + 1.0)
            - math.log(4.0 * math.pi)
            + math.lgamma(m + 0.5)
            - 0.5 * math.log(math.pi)
            - math.lgamma(m + 1.0)
        )
        table[m, m] = np.exp(start + m * log_sine)
        for l in range(m + 1, LMAX + 1):
            factor = math.sqrt((4.0 * l * l - 1.0) / (l * l - m * m))
            shrink = math.sqrt(((l - 1.0) ** 2 - m * m) / (4.0 * (l - 1.0) ** 2 - 1.0))
            before = table[m, l - 2] if l >= m + 2 else 0.0
            table[m, l] = factor * (cosine * table[m, l - 1] - shrink * before)
    return table


def unit_plan(devices):
    whole = LMAX // 2 * 2 - 1
    rows = 8
    while True:
        pairs = rows // 2 - 1
        left = max(0, whole - devices * pairs)
        if 2 + 2 * left <= devices:
            break
        rows += 8
    orders = np.zeros((devices, rows // 2), np.int32)
    units = {}
    for i in range(whole - left):
        d, j = i % devices, i // devices
        orders[d, j] = i + 1
        units[d * rows + 2 * j] = (i + 1, 0)
        units[d * rows + 2 * j + 1] = (i + 1, 1)
    singles = [(0, 0), (LMAX, 0)]
    for i in range(whole - left, whole):
        singles += [(i + 1, 0), (i + 1, 1)]
    for d, (m, p) in enumerate(singles):
        orders[d, pairs] = m
        units[d * rows + rows - 2] = (m, p)
    return rows, orders, units


def fourier_np(total, units, lon_count, lon_padded):
    forward = np.zeros((total, lon_padded))
    inverse = np.zeros((total, lon_padded))
    k = np.arange(lon_count)
    for at, (m, p) in units.items():
        angle = 2.0 * math.pi / lon_count * ((k * m) % lon_count)
        wave = np.cos(angle) if p == 0 else -np.sin(angle)
        doubling = 1.0 if m == 0 or 2 * m == lon_count else 2.0
        forward[at, :lon_count] = wave * (2.0 * math.pi / lon_count)
        inverse[at, :lon_count] = wave * doubling
    return forward.astype(np.float32), inverse.astype(np.float32)


def split_np(table):
    high = table.astype(ml_dtypes.bfloat16)
    low = (table - high.astype(np.float32)).astype(ml_dtypes.bfloat16)
    return jnp.asarray(high), jnp.asarray(low)


def split_x(table):
    high = lax.reduce_precision(table, 8, 7)
    return high.astype(BF16), (table - high).astype(BF16)


def split(value):
    high = value.astype(BF16)
    return high, (value - high.astype(F32)).astype(BF16)


def dot3(a, b):
    (ah, al), (bh, bl) = a, b
    dot = functools.partial(jnp.dot, preferred_element_type=F32)
    return dot(ah, bh) + (dot(ah, bl) + dot(al, bh))


def triple(value):
    high, low = split(value)
    return jnp.concatenate([high, high, low], axis=1)


def dot_triple(value, w_ref):
    w = w_ref[...].reshape(3 * w_ref.shape[1], w_ref.shape[2])
    return jnp.dot(triple(value), w, preferred_element_type=F32)


def params():
    return pltpu.CompilerParams(
        dimension_semantics=("arbitrary",), vmem_limit_bytes=VMEM_LIMIT
    )


def whole(shape):
    return pl.BlockSpec(shape, lambda i: (0,) * len(shape))


def diagonal(shape):
    return lax.broadcasted_iota(jnp.int32, shape, 1) == lax.broadcasted_iota(
        jnp.int32, shape, 2
    )


def analysis_body(shape, x, th_ref, tl_ref, o_ref):
    devices, rows, main = shape
    out = dot3((th_ref[...], tl_ref[...]), split(x))
    o_ref[...] = out[:, :main].reshape(devices, 1, rows, main)
    column = out[:, main : main + 1].reshape(devices, rows, 1)
    spare = jnp.where(diagonal((devices, rows, LANES)), column, 0.0).sum(axis=1)
    for d in range(devices):
        o_ref[d, 0, rows - 1 : rows, :LANES] = spare[d : d + 1, :]


def analysis_kernel(shape, x_ref, *refs):
    analysis_body(shape, x_ref[0], *refs)


def first_kernel(shape, part, state_ref, noise_ref, *refs):
    *tables, x_ref, o_ref, joined = refs
    lon, channels = state_ref.shape[1], state_ref.shape[3]
    base = channels // LANES * LANES

    @pl.when(pl.program_id(0) == 0)
    def _():
        joined[...] = jnp.zeros_like(joined)

    joined[:lon, :channels] = state_ref[0, :, part, :]
    lane = lax.broadcasted_iota(jnp.int32, noise_ref.shape[2:], 1)
    joined[:, base:] = jnp.where(lane < channels - base, joined[:, base:], noise_ref[0, 0])
    x = joined[...]
    x_ref[0] = x[:, : x_ref.shape[2]]
    analysis_body(shape, x, *tables, o_ref)


def analysis(x, first, row_count, table, plan, part=None):
    devices, rows, main = plan
    total, lon = table.shape
    th, tl = split_np(table)
    out_specs = [pl.BlockSpec((devices, 1, rows, main), lambda r: (0, r, 0, 0))]
    out_shape = [jax.ShapeDtypeStruct((devices, row_count, rows, main), F32)]
    scratch = []
    if part is None:
        kernel = functools.partial(analysis_kernel, plan)
        operands = [x]
        x_specs = [pl.BlockSpec((1, lon, main + 1), lambda r: (first + r, 0, 0))]
    else:
        kernel = functools.partial(first_kernel, plan, part)
        state, noise = operands = x
        x_specs = [
            pl.BlockSpec((1, *state.shape[1:]), lambda r: (r, 0, 0, 0)),
            pl.BlockSpec((1, 1, *noise.shape[2:]), lambda r: (part, r, 0, 0)),
        ]
        out_specs.insert(0, pl.BlockSpec((1, lon, main + 1), lambda r: (r, 0, 0)))
        out_shape.insert(0, jax.ShapeDtypeStruct((row_count, lon, main + 1), F32))
        scratch.append(pltpu.VMEM((lon, main + LANES), F32))
    return pl.pallas_call(
        kernel,
        grid=(row_count,),
        in_specs=x_specs + [whole((total, lon))] * 2,
        out_specs=out_specs,
        out_shape=out_shape,
        scratch_shapes=scratch,
        compiler_params=params(),
        cost_estimate=cost(1.2 * row_count),
        name="analysis",
    )(*operands, th, tl)


def synthesis_kernel(shape, joint, y_ref, th_ref, tl_ref, x_ref, *refs):
    devices, rows, main = shape
    *others, o_ref = refs
    total = devices * rows
    table = (th_ref[...], tl_ref[...])
    out = x_ref[0, :, :main] + dot3(table, split(y_ref[...].reshape(total, main)))
    if joint:
        lon, channels = o_ref.shape[1], o_ref.shape[3]
        for i, other in enumerate(others):
            o_ref[0, :, i, :] = other[0, :lon, :channels]
        o_ref[0, :, len(others), :] = out[:lon, :channels]
        return
    o_ref[0, :, :main] = out
    spare = y_ref[:, 0, rows - 1 : rows, :LANES]
    column = jnp.where(
        diagonal((devices, rows, LANES)), jnp.broadcast_to(spare, (devices, rows, LANES)), 0.0
    ).sum(axis=2, keepdims=True)
    column = jnp.broadcast_to(column.reshape(total, 1), (total, LANES))
    o_ref[0, :, main:] = x_ref[0, :, main:] + dot3(table, split(column))[:, :1]


def synthesis(y, table, x, first, held=None, joint=None):
    devices, row_count, rows, main = y.shape
    all_rows, lon, width = x.shape
    total = table.shape[0]
    th, tl = split_np(table.T.copy())
    x_spec = pl.BlockSpec((1, lon, width), lambda r: (first + r, 0, 0))
    operands = [y, th, tl, x]
    in_specs = [
        pl.BlockSpec((devices, 1, rows, main), lambda r: (0, r, 0, 0)),
        whole((lon, total)),
        whole((lon, total)),
        x_spec,
    ]
    out_spec, out_shape = x_spec, (all_rows, lon, width)
    aliases = {}
    if joint is not None:
        others, lon_out, channels = joint
        operands += others
        in_specs += [x_spec] * len(others)
        out_shape = (all_rows, lon_out, len(others) + 1, channels)
        out_spec = pl.BlockSpec((1, *out_shape[1:]), lambda r: (r, 0, 0, 0))
    elif held is not None:
        aliases = {len(operands): 0}
        operands.append(held)
        in_specs.append(pl.BlockSpec(memory_space=pl.ANY))
    return pl.pallas_call(
        functools.partial(synthesis_kernel, (devices, rows, main), joint is not None),
        grid=(row_count,),
        in_specs=in_specs,
        out_specs=out_spec,
        out_shape=jax.ShapeDtypeStruct(out_shape, F32),
        input_output_aliases=aliases,
        compiler_params=params(),
        cost_estimate=cost(1.2 * row_count),
        name="synthesis",
    )(*operands)


def halves(chains, rows):
    steps = len(chains[0][3])
    sizes = [rows >> k for k in range(steps + 1)]
    sides, starts = [], []
    for *_, order in chains:
        side, at = [], [0]
        for k, (axis, bit_at) in enumerate(order):
            me = lax.axis_index(axis)
            bit = (me // (1 << bit_at)) % 2
            side.append((bit, {axis: me + (1 - 2 * bit) * (1 << bit_at)}))
            at.append(at[-1] + bit * sizes[k + 1])
        sides.append(side)
        starts.append(at)
    return sides, starts, sizes


def greet(partners):
    barrier = pltpu.get_barrier_semaphore()
    for _, partner in partners:
        pl.semaphore_signal(
            barrier, inc=1, device_id=partner, device_id_type=pl.DeviceIdType.MESH
        )
    pl.semaphore_wait(barrier, len(partners))


def send_to(partner, source, target, send, recv):
    return pltpu.make_async_remote_copy(
        src_ref=source,
        dst_ref=target,
        send_sem=send,
        recv_sem=recv,
        device_id=partner,
        device_id_type=pl.DeviceIdType.MESH,
    )


def scatter_sum_kernel(chains, near, arrays, *refs):
    count, steps = len(chains), len(chains[0][3])
    ins, outs, refs = refs[:arrays], refs[arrays : 2 * arrays], refs[2 * arrays :]
    send, recv = refs[-2:]
    kept, landed = refs[:count], refs[count:-2]
    sides, starts, sizes = halves(chains, ins[0].shape[0])
    lanes = [pl.ds(first, size) for _, first, size, _ in chains]
    greet(sides[0])

    def halve(c, k):
        bit, partner = sides[c][k]
        give = starts[c][k] + (1 - bit) * sizes[k + 1]
        give = pl.ds(pl.multiple_of(give, 8), sizes[k + 1])
        source = ins[chains[c][0]].at[give, lanes[c]] if k == 0 else kept[c].at[give]
        return send_to(partner, source, landed[c * steps + k], send.at[c, k], recv.at[c, k])

    def share(c, k):
        return pl.ds(pl.multiple_of(starts[c][k] - starts[c][near], 8), sizes[k])

    def double(c, k):
        have = outs[chains[c][0]].at[share(c, k + 1), lanes[c]]
        step = 2 * steps - 1 - k
        return send_to(sides[c][k][1], have, have, send.at[c, step], recv.at[c, step])

    flying = []
    for c in range(count):
        flying.append(halve(c, 0))
        flying[c].start()
    for k in range(steps):
        for c in range(count):
            flying[c].wait()
            rows = pl.ds(pl.multiple_of(starts[c][k + 1], 8), sizes[k + 1])
            mine = ins[chains[c][0]][rows, lanes[c]] if k == 0 else kept[c][rows, :]
            total = mine + landed[c * steps + k][...]
            if k + 1 < steps:
                kept[c][rows, :] = total
                flying[c] = halve(c, k + 1)
            else:
                outs[chains[c][0]][share(c, steps), lanes[c]] = total
                flying[c] = double(c, k)
            flying[c].start()
    for k in reversed(range(near, steps)):
        for c in range(count):
            flying[c].wait()
            if k > near:
                flying[c] = double(c, k - 1)
                flying[c].start()


def gather_kernel(chains, near, arrays, *refs):
    count = len(chains)
    ins, outs, (send, recv) = refs[:arrays], refs[arrays : 2 * arrays], refs[2 * arrays :]
    sides, starts, sizes = halves(chains, outs[0].shape[0])
    lanes = [pl.ds(first, size) for _, first, size, _ in chains]
    greet(sides[0][:near])

    def double(c, k):
        rows = pl.ds(pl.multiple_of(starts[c][k + 1], 8), sizes[k + 1])
        have = outs[chains[c][0]].at[rows, lanes[c]]
        return send_to(sides[c][k][1], have, have, send.at[c, k], recv.at[c, k])

    flying = []
    for c in range(count):
        rows = pl.ds(pl.multiple_of(starts[c][near], 8), sizes[near])
        outs[chains[c][0]][rows, lanes[c]] = ins[chains[c][0]][:, lanes[c]]
        flying.append(double(c, near - 1))
        flying[c].start()
    for k in reversed(range(near)):
        for c in range(count):
            flying[c].wait()
            if k > 0:
                flying[c] = double(c, k - 1)
                flying[c].start()


def lane_chains(arrays, width, orders):
    cut = width // (2 * LANES) * LANES
    both = ((0, cut, orders[0]), (cut, width - cut, orders[1]))
    return [(i, *half) for i in range(arrays) for half in both]


def remote_params(collective_id):
    return pltpu.CompilerParams(
        collective_id=collective_id, has_side_effects=True, vmem_limit_bytes=VMEM_LIMIT
    )


def scatter_sum(xs, orders, near, collective_id):
    rows, width = xs[0].shape
    steps = len(orders[0])
    chains = lane_chains(len(xs), width, orders)
    vmem = pl.BlockSpec(memory_space=pltpu.VMEM)
    return pl.pallas_call(
        functools.partial(scatter_sum_kernel, chains, near, len(xs)),
        in_specs=[vmem] * len(xs),
        out_specs=[vmem] * len(xs),
        out_shape=[jax.ShapeDtypeStruct((rows >> near, width), F32)] * len(xs),
        scratch_shapes=[pltpu.VMEM((rows, size), F32) for _, _, size, _ in chains]
        + [
            pltpu.VMEM((rows >> (k + 1), size), F32)
            for _, _, size, _ in chains
            for k in range(steps)
        ]
        + [pltpu.SemaphoreType.DMA((len(chains), 2 * steps))] * 2,
        compiler_params=remote_params(collective_id),
        cost_estimate=cost(80),
        name="scatter_sum",
    )(*xs)


def gather(xs, orders, near, collective_id):
    rows, width = xs[0].shape
    chains = lane_chains(len(xs), width, orders)
    vmem = pl.BlockSpec(memory_space=pltpu.VMEM)
    return pl.pallas_call(
        functools.partial(gather_kernel, chains, near, len(xs)),
        in_specs=[vmem] * len(xs),
        out_specs=[vmem] * len(xs),
        out_shape=[jax.ShapeDtypeStruct((rows << near, width), F32)] * len(xs),
        scratch_shapes=[pltpu.SemaphoreType.DMA((len(chains), near))] * 2,
        compiler_params=remote_params(collective_id),
        cost_estimate=cost(40),
        name="gather",
    )(*xs)


def weights_kernel(hidden, main, a_ref, b_ref, *refs):
    for w_ref, (plain, flipped, e) in zip((a_ref, b_ref), (refs[:3], refs[3:])):
        w = w_ref[...]
        column = lax.broadcasted_iota(jnp.int32, w.shape, 1) + pl.program_id(0) * LANES
        w = jnp.where(column < hidden, w, 0.0)
        for ref, value in ((plain, w[:main]), (flipped, w[:main].T)):
            high, low = split(value)
            ref[0] = high
            ref[1] = low
            ref[2] = high
        e[...] = w[main : main + 1]


def prepare_weights(a, b):
    width, hidden = a.shape
    main = width // LANES * LANES
    tiles = (hidden + LANES - 1) // LANES
    across = pl.BlockSpec((3, main, LANES), lambda i: (0, 0, i))
    down = pl.BlockSpec((3, LANES, main), lambda i: (0, i, 0))
    row = pl.BlockSpec((1, LANES), lambda i: (0, i))
    total = tiles * LANES
    shapes = [
        jax.ShapeDtypeStruct((3, main, total), BF16),
        jax.ShapeDtypeStruct((3, total, main), BF16),
        jax.ShapeDtypeStruct((1, total), F32),
    ]
    out = pl.pallas_call(
        functools.partial(weights_kernel, hidden, main),
        grid=(tiles,),
        in_specs=[pl.BlockSpec((width, LANES), lambda i: (0, i))] * 2,
        out_specs=[across, down, row] * 2,
        out_shape=shapes * 2,
        compiler_params=params(),
        cost_estimate=cost(12),
        name="weights",
    )(a, b)
    return out[:3], out[3:]


def lane_mask(shape, j):
    lane = lax.broadcasted_iota(jnp.int32, shape, 1)
    return (lane == 2 * j) | (lane == 2 * j + 1)


def filter_kernel(shape, backward, *refs):
    in_sizes, out_sizes, rows = shape
    g_refs, refs = refs[: len(in_sizes)], refs[len(in_sizes) :]
    ah_ref, al_ref, bh_ref, bl_ref, gain_ref, egain_ref = refs[:6]
    refs = refs[6:]
    if backward:
        c_ref, ec_ref = refs[:2]
        refs = refs[2:]
    h_refs, refs = refs[: len(out_sizes)], refs[len(out_sizes) :]
    if backward:
        gg_ref, egg_ref = refs
    else:
        c_ref, ec_ref = refs
    tables = rows // 2
    slots = sum(out_sizes)

    def load(u):
        parts = [
            ref[pl.ds(u, n, stride=rows), :] for ref, n in zip(g_refs, in_sizes)
        ]
        return parts[0] if len(parts) == 1 else jnp.concatenate(parts, axis=0)

    def store(u, value):
        first = 0
        for ref, n in zip(h_refs, out_sizes):
            ref[pl.ds(u, n, stride=rows), :] = value[first : first + n, :]
            first += n

    gain = gain_ref[...]
    gain2 = jnp.concatenate([gain, gain], axis=1)
    total = jnp.zeros(gain.shape, F32)
    for j in range(tables):
        x = jnp.concatenate([load(2 * j), load(2 * j + 1)], axis=1)
        c = dot3((ah_ref[j], al_ref[j]), split(x))
        if backward:
            total += c_ref[2 * j] * c[:, :LANES]
            if j < tables - 1:
                total += c_ref[2 * j + 1] * c[:, LANES:]
        else:
            c_ref[2 * j] = c[:, :LANES]
            c_ref[2 * j + 1] = c[:, LANES:]
        y = dot3((bh_ref[j], bl_ref[j]), split(c * gain2))
        store(2 * j, y[:, :LANES])
        store(2 * j + 1, y[:, LANES:])
    if backward:
        gg_ref[...] = total

    @pl.when(pl.program_id(0) == 0)
    def _():
        x = split(load(rows - 1))
        c = jnp.zeros(gain.shape, F32)
        for j in range(tables):
            mine = dot3((ah_ref[j], al_ref[j]), x)
            c = jnp.where(lane_mask(c.shape, j), mine, c)
        if backward:
            egg_ref[...] = ec_ref[...] * c
        else:
            ec_ref[...] = c
        c = split(c * egain_ref[...])
        y = jnp.zeros((slots, LANES), F32)
        for j in range(tables):
            mine = dot3((bh_ref[j], bl_ref[j]), c)
            y = jnp.where(lane_mask(y.shape, j), mine, y)
        store(rows - 1, y)


def filter_slots(gs, first, second, gain, out_rows, coeffs=None):
    devices, _, rows, main = gs[0].shape
    in_sizes = [devices * g.shape[1] for g in gs]
    out_sizes = [devices * n for n in out_rows]
    slots = sum(in_sizes)
    degrees = first[0].shape[1]
    backward = coeffs is not None
    block = lambda n: pl.BlockSpec((n * rows, LANES), lambda t: (0, t))
    c_spec = pl.BlockSpec((rows, degrees, LANES), lambda t: (0, 0, t))
    ec_spec = whole((degrees, LANES))
    gg_spec = pl.BlockSpec((degrees, LANES), lambda t: (0, t))
    main_gain, extra_gain = gain
    in_specs = [block(n) for n in in_sizes] + [
        whole(first[0].shape),
        whole(first[0].shape),
        whole(second[0].shape),
        whole(second[0].shape),
        gg_spec,
        whole((degrees, 1)),
    ]
    operands = [g.reshape(-1, main) for g in gs]
    operands += [*first, *second, main_gain, extra_gain]
    out_shape = [jax.ShapeDtypeStruct((n * rows, main), F32) for n in out_sizes]
    out_specs = [block(n) for n in out_sizes]
    if backward:
        in_specs += [c_spec, ec_spec]
        operands += list(coeffs)
        out_shape.append(jax.ShapeDtypeStruct((degrees, main), F32))
        out_specs.append(gg_spec)
    else:
        out_shape.append(jax.ShapeDtypeStruct((rows, degrees, main), F32))
        out_specs.append(c_spec)
    out_shape.append(jax.ShapeDtypeStruct((degrees, LANES), F32))
    out_specs.append(ec_spec)
    *h, c, ec = pl.pallas_call(
        functools.partial(filter_kernel, (in_sizes, out_sizes, rows), backward),
        grid=(main // LANES,),
        in_specs=in_specs,
        out_specs=out_specs,
        out_shape=out_shape,
        compiler_params=params(),
        cost_estimate=cost(12),
        name="filter_back" if backward else "filter",
    )(*operands)
    h = [x.reshape(devices, n, rows, main) for x, n in zip(h, out_rows)]
    return h, (c, ec)


def mlp_kernel(main, m_ref, w1, w1e, b1, w2, w2e, b2, b2e, *refs):
    act_ref, slope_ref, out_ref, field_ref = refs[-4:]
    m = m_ref[:, :main]
    extra = m_ref[:, main:]
    v = dot_triple(m, w1) + extra * w1e[...] + b1[...]
    cdf = 0.5 * (1.0 + lax.erf(v * (1.0 / math.sqrt(2.0))))
    slope_ref[...] = cdf + v * jnp.exp(-0.5 * v * v) * (1.0 / math.sqrt(2.0 * math.pi))
    act = v * cdf
    act_ref[...] = act
    out = m + dot_triple(act, w2) + b2[...]
    out_ref[:, :main] = out
    field_ref[...] = out
    last = jnp.sum(act * w2e[...], axis=1, keepdims=True)
    out_ref[:, main:] = extra + last + b2e[...]


def tile_of(tokens, most):
    tile = most // 8 * 8
    while tokens % tile:
        tile -= 8
    return tile


def mlp(mixed, first, tokens, weights, held):
    whole_count, width = mixed.shape
    w1, w1e, b1, w2, w2e, b2, b2e = weights
    _, main, hidden = w1.shape
    tile = tile_of(math.gcd(first, tokens), 368)
    at = first // tile
    row = lambda n: pl.BlockSpec((tile, n), lambda i: (at + i, 0))
    shape = lambda n: jax.ShapeDtypeStruct((whole_count, n), F32)
    operands = [mixed, w1, w1e, b1, w2, w2e, b2, b2e]
    in_specs = [row(width)] + [whole(x.shape) for x in operands[1:]]
    aliases = {len(operands) + i: i for i in range(len(held))}
    return pl.pallas_call(
        functools.partial(mlp_kernel, main),
        grid=(tokens // tile,),
        in_specs=in_specs + [pl.BlockSpec(memory_space=pl.ANY)] * len(held),
        out_specs=(
            row(hidden),
            row(hidden),
            row(width),
            pl.BlockSpec((tile, main), lambda i: (i, 0)),
        ),
        out_shape=(
            shape(hidden),
            shape(hidden),
            shape(width),
            jax.ShapeDtypeStruct((tokens, main), F32),
        ),
        input_output_aliases=aliases,
        compiler_params=params(),
        cost_estimate=cost(0.023 * tokens),
        name="mlp",
    )(*operands, *held)


def mlp_back_kernel(main, g_ref, slope_ref, w2, w1, w1e, *refs):
    pre_ref, gm_ref, bias_in_ref, bias_out_ref = refs[-4:]

    @pl.when(pl.program_id(0) == 0)
    def _():
        bias_in_ref[...] = jnp.zeros_like(bias_in_ref)
        bias_out_ref[...] = jnp.zeros_like(bias_out_ref)

    g = g_ref[...]
    pre = dot_triple(g, w2) * slope_ref[...]
    pre_ref[...] = pre
    gm_ref[:, :main] = g + dot_triple(pre, w1)
    gm_ref[:, main:] = jnp.sum(pre * w1e[...], axis=1, keepdims=True)
    bias_in_ref[...] += jnp.sum(pre, axis=0, keepdims=True)
    bias_out_ref[...] += jnp.sum(g, axis=0, keepdims=True)


def mlp_back(g, slope, first, weights, held):
    tokens, main = g.shape
    whole_count, hidden = slope.shape
    w2, w1, w1e = weights
    tile = tile_of(math.gcd(first, tokens), 368)
    at = first // tile
    row = lambda n: pl.BlockSpec((tile, n), lambda i: (at + i, 0))
    shape = lambda n: jax.ShapeDtypeStruct((whole_count, n), F32)
    operands = [g, slope, w2, w1, w1e]
    in_specs = [pl.BlockSpec((tile, main), lambda i: (i, 0)), row(hidden)]
    in_specs += [whole(x.shape) for x in operands[2:]]
    aliases = {len(operands) + i: i for i in range(len(held))}
    return pl.pallas_call(
        functools.partial(mlp_back_kernel, main),
        grid=(tokens // tile,),
        in_specs=in_specs + [pl.BlockSpec(memory_space=pl.ANY)] * len(held),
        out_specs=(row(hidden), row(main + 1), whole((1, hidden)), whole((1, main))),
        out_shape=(
            shape(hidden),
            shape(main + 1),
            jax.ShapeDtypeStruct((1, hidden), F32),
            jax.ShapeDtypeStruct((1, main), F32),
        ),
        input_output_aliases=aliases,
        compiler_params=params(),
        cost_estimate=cost(0.021 * tokens),
        name="mlp_back",
    )(*operands, *held)


def crps_kernel(shape, groups_ref, *refs):
    own, sources, lane_tiles, channels = shape
    members = own * sources
    f_refs = refs[:members]
    t_ref, a_ref = refs[members : members + 2]
    g_refs = refs[members + 2 : 2 * members + 2]
    loss_ref, f_all, g_all = refs[2 * members + 2 :]
    pair_scale = 1.0 / (ENSEMBLE_SIZE * (ENSEMBLE_SIZE - 1))

    @pl.when(pl.program_id(0) == 0)
    def _():
        loss_ref[...] = jnp.zeros_like(loss_ref)

    def chunk(i, total):
        rows = pl.ds(pl.multiple_of(i * 8, 8), 8)
        area = jnp.broadcast_to(a_ref[rows, :], (8, LANES))
        for j in range(lane_tiles):
            lanes = slice(j * LANES, (j + 1) * LANES)
            weight = area
            if (j + 1) * LANES > channels:
                lane = lax.broadcasted_iota(jnp.int32, area.shape, 1)
                weight = jnp.where(lane + j * LANES < channels, area, 0.0)
            for source in range(sources):
                for b in range(own):
                    f_all[source * own + b] = f_refs[source * own + b][rows, lanes]
            for d in range(DATES):
                places = [groups_ref[d * ENSEMBLE_SIZE + i] for i in range(ENSEMBLE_SIZE)]
                f = [f_all[m] for m in places]
                observed = t_ref[d, rows, lanes]
                skill = jnp.zeros_like(area)
                couple = jnp.zeros_like(area)
                grads = []
                for v in f:
                    v = v - observed
                    square = v * v + 1.0
                    inverse = lax.rsqrt(square)
                    skill += square * inverse
                    grads.append(v * inverse * (1.0 / ENSEMBLE_SIZE))
                for m in range(ENSEMBLE_SIZE):
                    for n in range(m + 1, ENSEMBLE_SIZE):
                        v = f[m] - f[n]
                        square = v * v + 1.0
                        inverse = lax.rsqrt(square)
                        couple += square * inverse
                        v = v * inverse * pair_scale
                        grads[m] -= v
                        grads[n] += v
                total += weight * (skill * (1.0 / ENSEMBLE_SIZE) - couple * pair_scale)
                for m, grad in zip(places, grads):
                    g_all[m] = weight * grad
            for source in range(sources):
                for b in range(own):
                    g_refs[source * own + b][rows, lanes] = g_all[source * own + b]
        return total

    count = a_ref.shape[0] // 8
    loss_ref[...] += lax.fori_loop(0, count, chunk, jnp.zeros((8, LANES), F32))


def crps(fields, own, observed, area, places, channels):
    members = len(fields)
    points, main = fields[0].shape
    tile = points // 2 if points % 16 == 0 else points
    spec = pl.BlockSpec((tile, main), lambda i, g: (i, 0))
    *grads, loss = pl.pallas_call(
        functools.partial(crps_kernel, (own, members // own, main // LANES, channels)),
        grid_spec=pltpu.PrefetchScalarGridSpec(
            num_scalar_prefetch=1,
            grid=(points // tile,),
            in_specs=[spec] * members
            + [
                pl.BlockSpec((DATES, tile, main), lambda i, g: (0, i, 0)),
                pl.BlockSpec((tile, 1), lambda i, g: (i, 0)),
            ],
            out_specs=[spec] * members + [pl.BlockSpec((8, LANES), lambda i, g: (0, 0))],
            scratch_shapes=[pltpu.VMEM((members, 8, LANES), F32)] * 2,
        ),
        out_shape=[jax.ShapeDtypeStruct((points, main), F32)] * members
        + [jax.ShapeDtypeStruct((8, LANES), F32)],
        compiler_params=params(),
        cost_estimate=cost(0.045 * points),
        name="crps",
    )(places, *fields, observed, area)
    return grads, jnp.sum(loss)


def local(
    state_now,
    sample_random_maps,
    noise_scale,
    spec_gain,
    weight_in,
    bias_in,
    weight_out,
    bias_out,
    targets,
    date_of,
    row_slot,
):
    highest, high = lax.Precision.HIGHEST, lax.Precision.HIGH
    own, row_count, lon, channels = state_now.shape
    width, hidden = weight_in.shape
    main = width // LANES * LANES
    devices = lax.axis_size("lat")
    sources = lax.axis_size("member")
    lat_rank = lax.axis_index("lat")
    member_rank = lax.axis_index("member")
    slots = devices * row_count
    members = own * sources

    groups = [row_count // 3] * 3 if row_count % 3 == 0 else [row_count]
    starts = [sum(groups[:q]) for q in range(len(groups))]
    padded = (lon + 7) // 8 * 8
    while any(n * padded % (8 * sources) for n in groups):
        padded += 8
    points = [n * padded // sources for n in groups]

    rows, orders, units = unit_plan(devices)
    plan = (devices, rows, main)
    forward_table, inverse_table = fourier_np(devices * rows, units, lon, padded)
    degrees = (LMAX + 8) // 8 * 8
    full = np.zeros((LMAX + 1, degrees, NLAT), np.float32)
    full[:, : LMAX + 1] = legendre_np().astype(np.float32)
    mine = lax.dynamic_index_in_dim(jnp.asarray(full[orders]), lat_rank, 0, keepdims=False)
    sine = np.sin((np.arange(NLAT) + 0.5) * (math.pi / NLAT))
    geometry = jnp.asarray(
        np.stack(
            [np.ones(NLAT), math.pi / NLAT * sine, NLAT * sine / np.sum(sine)]
        ).astype(np.float32)
    )

    def low_tables(blocks):
        ids = np.arange(slots, dtype=np.int32).reshape(devices, row_count)
        ids = np.concatenate([ids[:, a : a + n].reshape(-1) for a, n in blocks])
        hits = (row_slot[:, None] == jnp.asarray(ids)[None, :]).astype(F32)
        quadrature = jnp.dot(geometry, hits, precision=highest)[1]
        table = jnp.einsum("jla,as->jls", mine, hits, precision=highest)
        weighted, plain = split_x(table * quadrature), split_x(table)
        flip = lambda pair: tuple(jnp.swapaxes(t, 1, 2) for t in pair)
        return weighted, plain, flip(weighted), flip(plain)

    in_full = low_tables([(0, row_count)])
    in_groups = low_tables(list(zip(starts, groups)))

    own_ids = lat_rank * row_count + jnp.arange(row_count, dtype=jnp.int32)
    hits_own = (row_slot[:, None] == own_ids[None, :]).astype(F32)
    used_own, _, area_own = jnp.dot(geometry, hits_own, precision=highest)
    gain = jnp.pad(spec_gain, ((0, degrees - LMAX - 1), (0, 0)))
    gain = (gain[:, :main], gain[:, main:])

    hidden_padded = (hidden + LANES - 1) // LANES * LANES
    pad_cols = lambda w: jnp.pad(w, ((0, 0), (0, hidden_padded - hidden)))
    w1_parts, w2t_parts = prepare_weights(weight_in, weight_out.T)
    forward_weights = (
        w1_parts[0],
        w1_parts[2],
        pad_cols(bias_in[None, :]),
        w2t_parts[1],
        w2t_parts[2],
        bias_out[None, :main],
        bias_out[None, main:],
    )
    backward_weights = (w2t_parts[0], w1_parts[1], w1_parts[2])

    base = channels // LANES * LANES
    noise = jnp.pad(
        noise_scale[:, None, None, :] * sample_random_maps,
        ((0, 0), (0, 0), (0, padded - lon), (channels - base, main + LANES - width)),
    )
    state = jnp.transpose(state_now, (1, 2, 0, 3))
    observed = jnp.pad(
        targets, ((0, 0), (0, 0), (0, padded - lon), (0, main - channels))
    )
    token_area = jnp.where(jnp.arange(padded)[None, :] < lon, area_own[:, None], 0.0)
    observed_share, area_share = [], []
    for a, n, size in zip(starts, groups, points):
        o = observed[:, a : a + n].reshape(DATES, n * padded, main)
        o = lax.dynamic_slice_in_dim(o, member_rank * size, size, axis=1)
        t = token_area[a : a + n].reshape(n * padded, 1)
        t = lax.dynamic_slice_in_dim(t, member_rank * size, size, axis=0)
        observed_share.append(o)
        area_share.append(t)
    by_date = jnp.argsort(date_of, stable=True).astype(jnp.int32)
    places = ((by_date // own) ^ member_rank) * own + by_date % own

    def tie(x, *tokens):
        return lax.optimization_barrier((x, tokens))[0]

    moved = []

    def to_owner(x):
        x = tie(x, *moved[-1:])
        moved.append(lax.all_to_all(x, "lat", split_axis=0, concat_axis=0, tiled=True))
        return moved[-1]

    def swap(x, distance):
        if distance == 0:
            return x
        pairs = [(i, i ^ distance) for i in range(sources)]
        return lax.ppermute(x, "member", pairs)

    def exchange(q, field):
        size = points[q]
        shares = []
        for distance in range(sources):
            share = lax.dynamic_slice_in_dim(
                field, (member_rank ^ distance) * size, size, axis=0
            )
            shares.append(swap(share, distance))
        return shares

    every = range(len(groups))
    final = own - 1

    inputs, spectra, synths, coeffs = [], [], [], []
    for b in range(own):
        if b > 0:
            state, noise = tie((state, noise), f)
        x, f = analysis((state, noise), 0, row_count, forward_table, plan, b)
        inputs.append(x)
        spectra.append(to_owner(f))
    prepared = (forward_weights, backward_weights, observed_share, area_share, places)
    for b in range(own):
        if b > 0:
            spectra[b] = tie(spectra[b], *h)
        if b == final:
            spectra[b], prepared = lax.optimization_barrier((spectra[b], prepared))
        h, c = filter_slots(
            [spectra[b]],
            in_full[0],
            in_groups[3] if b == final else in_full[3],
            gain,
            groups if b == final else [row_count],
        )
        coeffs.append(c)
        synths.append([to_owner(h[0])])
    forward_weights, backward_weights, observed_share, area_share, places = prepared

    mixed, held, shares = [None] * own, [[] for _ in range(own)], {}

    def mix(b, q, *tokens):
        first, y = (starts[q], synths[b][q]) if b == final else (0, synths[b][0])
        y = tie(y, *tokens)
        mixed[b] = synthesis(y, inverse_table, inputs[b], first, mixed[b])

    def forward(b, q, *tokens):
        m = tie(mixed[b], *tokens).reshape(row_count * padded, width)
        *held[b], field = mlp(
            m, starts[q] * padded, groups[q] * padded, forward_weights, held[b]
        )
        shares[b, q] = exchange(q, field)
        return field

    results, got = {}, {}
    losses = []

    def score(q, *tokens):
        fields = [shares[b, q][d] for d in range(sources) for b in range(own)]
        fields = tie(fields, *tokens)
        out, part = crps(fields, own, observed_share[q], area_share[q], places, channels)
        losses.append(part)
        results[q] = out
        got[0, q] = returned(0, q)
        return out[0]

    def returned(b, q):
        return [swap(results[q][d * own + b], d) for d in range(sources)]

    def gradient(b, parts):
        size = sum(groups[q] for q in parts) * padded
        g = jnp.zeros((size, main), F32)
        for q in parts:
            for distance, share in enumerate(got[b, q]):
                at = (member_rank ^ distance) * points[q]
                at += (starts[q] - starts[parts[0]]) * padded
                g = lax.dynamic_update_slice_in_dim(g, share, at, axis=0)
        return g

    grads = [[] for _ in range(own)]
    slopes, back_held = {}, [[] for _ in range(own)]
    bias_in_sums, bias_out_sums = [], []
    back = [[] for _ in range(own)]

    def backward(b, q, *tokens):
        g = tie(gradient(b, [q]), *tokens)
        *back_held[b], b1, b2 = mlp_back(
            g, held[b][1], starts[q] * padded, backward_weights, back_held[b]
        )
        grads[b].append(g)
        bias_in_sums.append(b1)
        bias_out_sums.append(b2)
        return b2

    def send_back(b, parts):
        gm = tie(back_held[b][1], *moved[-1:]) if b > 0 or parts[0] > 0 else back_held[b][1]
        gm = gm.reshape(row_count, padded, width)
        size = sum(groups[q] for q in parts)
        f = analysis(gm, starts[parts[0]], size, inverse_table, plan)[0]
        back[b].append(to_owner(f))
        return f

    token = ()
    in_turns = len(groups) == 3
    for b in range(final):
        mix(b, 0, *token)
        for q in every:
            if in_turns and b == final - 1 and q == 2:
                break
            token = (forward(b, q, *token),)
    if in_turns:
        synths[final].append(to_owner(tie(h[1], *token)))
        mix(final, 0, *token)
        token = (forward(final, 0),)
        synths[final].append(to_owner(tie(h[2], *token)))
        token = (forward(final - 1, 2, *token),)
        token = (score(0, *token),)
        mix(final, 1, *token)
        token = (forward(final, 1),)
        backward(0, 0, *token)
        token = (send_back(0, [0]),)
        token = (score(1, *token),)
        mix(final, 2, *token)
        token = (forward(final, 2),)
        backward(0, 1, *token)
        token = (send_back(0, [1]),)
        for b in range(1, own):
            results[0] = tie(results[0], *token)
            got[b, 0] = returned(b, 0)
        token = (score(2, *token),)
        for b in range(1, own):
            token = (backward(b, 0, *token),)
            results[1] = tie(results[1], got[0, 2])
            got[b, 1] = returned(b, 1)
            results[2] = tie(results[2], got[b, 1])
            got[b, 2] = returned(b, 2)
        backward(0, 2, *token)
        token = (send_back(0, [2]),)
        for b in range(1, own):
            token = (backward(b, 1, *token),)
            token = (backward(b, 2, *token),)
            token = (send_back(b, list(every)),)
    else:
        for q in every:
            mix(final, q, *token)
            token = (forward(final, q),)
        for q in every:
            token = (score(q, *token),)
        for b in range(own):
            for q in every:
                if b > 0:
                    got[b, q] = returned(b, q)
                token = (backward(b, q, *token),)
            token = (send_back(b, list(every)),)
    loss = sum(losses)
    mixed = [m.reshape(row_count * padded, width) for m in mixed]
    act = [h[0] for h in held]
    block = [h[2] for h in held]
    g_pre = [h[0] for h in back_held]
    g_mixed = [h[1] for h in back_held]

    grads = tie(grads, *token)
    grad_out_t = 0.0
    for b in range(own):
        at = 0
        for g in grads[b]:
            n = g.shape[0]
            grad_out_t += jnp.einsum("tc,th->ch", g, act[b][at : at + n], precision=high)
            at += n
    g_pre = tie(g_pre, *token)
    grad_in = sum(
        jnp.einsum("tc,th->ch", mixed[b], g_pre[b], precision=high) for b in range(own)
    )
    grad_bias_in = sum(bias_in_sums)[0, :hidden]
    grad_bias_out = jnp.pad(sum(bias_out_sums)[0], (0, width - main))

    back[0], grad_out_t, grad_in = lax.optimization_barrier((back[0], grad_out_t, grad_in))
    spreads = []
    gain_by_member = []
    for b in range(own):
        split_in = len(back[b]) > 1
        (h,), (gg, egg) = filter_slots(
            back[b],
            in_groups[1] if split_in else in_full[1],
            in_full[2],
            gain,
            [row_count],
            coeffs[b],
        )
        if b == final:
            last_filtered = h
        else:
            spreads.append(to_owner(h))
        low = jnp.concatenate([gg, jnp.sum(egg, axis=1, keepdims=True)], axis=1)
        gain_by_member.append(low[: LMAX + 1])
    grad_gain = sum(gain_by_member)

    scale_parts = []
    for b in range(own):
        gm = g_mixed[b].reshape(row_count, padded, width)[:, :lon, channels:]
        direct = jnp.sum(gm * sample_random_maps[b], axis=(0, 1))
        spectral = jnp.sum(
            spec_gain[:, channels:] * gain_by_member[b][:, channels:], axis=0
        )
        scale_parts.append(direct + spectral / noise_scale[b])
    noise_count = width - channels
    scale_row = lax.dynamic_update_slice(
        jnp.zeros((members * noise_count,), F32),
        jnp.concatenate(scale_parts),
        (member_rank * own * noise_count,),
    )
    line = lambda v: jnp.pad(v, (0, -v.shape[0] % width)).reshape(-1, width)
    small = [grad_bias_out, grad_bias_in, jnp.concatenate([loss[None], scale_row])]
    small = [line(v) for v in small]
    pack = jnp.concatenate([grad_gain] + small, axis=0)
    bits = [("lat", 0), ("member", 0), ("member", 1)]
    bits += [("lat", k) for k in range(1, devices.bit_length() - 1)]
    if sources == 4 and len(bits) <= 5:
        lanes = hidden_padded
        flat = pack.reshape(-1)
        flat = jnp.pad(flat, (0, -flat.shape[0] % lanes)).reshape(-1, lanes)
        unit = 8 << len(bits)
        size = -(-(width + flat.shape[0]) // unit) * unit
        first = jnp.concatenate([grad_in, flat])
        arrays = [jnp.pad(x, ((0, size - x.shape[0]), (0, 0))) for x in (first, grad_out_t)]
        orders = [bits, [bits[0], bits[2], bits[1]] + bits[3:]]
        arrays = scatter_sum(tie(arrays, last_filtered), orders, 3, 1)
        last_filtered, arrays = lax.optimization_barrier((last_filtered, arrays))
        arrays = gather(tie(arrays, *spreads), orders, 3, 2)
        block, (first, second) = lax.optimization_barrier((block, arrays))
        grad_in, grad_out_t = first[:width, :hidden], second[:main, :hidden]
        flat = first[width : width + flat.shape[0]].reshape(-1)
        pack = flat[: pack.size].reshape(pack.shape)
    else:
        grad_in, grad_out_t, pack = lax.psum(
            (grad_in[:, :hidden], grad_out_t[:, :hidden], pack), ("member", "lat")
        )
    layer_output = jnp.stack(
        [x.reshape(row_count, padded, width)[:, :lon] for x in block]
    ) * used_own[None, :, None, None]
    done = []
    spreads.append(to_owner(last_filtered))
    for b in range(own):
        done.append(
            synthesis(
                tie(spreads[b], *done),
                forward_table,
                g_mixed[b].reshape(row_count, padded, width),
                0,
                joint=(done, lon, channels) if b == final else None,
            )
        )
    grad_state = jnp.transpose(done[-1], (2, 0, 1, 3))
    at = LMAX + 1
    grad_gain = pack[:at]
    grad_bias_out = pack[at]
    after = at + 1 + small[1].shape[0]
    grad_bias_in = pack[at + 1 : after].reshape(-1)[:hidden]
    last_row = pack[after:].reshape(-1)
    crps_loss = last_row[0] / (DATES * NLAT * NLON * channels)
    grad_scale = lax.dynamic_slice_in_dim(
        last_row, 1 + member_rank * own * noise_count, own * noise_count
    ).reshape(own, noise_count)
    grad_weight_out = jnp.pad(grad_out_t, ((0, width - main), (0, 0))).T

    return (
        crps_loss,
        layer_output,
        grad_state,
        grad_scale,
        grad_gain,
        grad_in,
        grad_bias_in,
        grad_weight_out,
        grad_bias_out,
    )


def solution(mesh):
    return jax.shard_map(
        local,
        mesh=mesh,
        in_specs=(
            P("member", "lat", None, None),
            P("member", "lat", None, None),
            P("member", None),
            P(),
            P(),
            P(),
            P(),
            P(),
            P(None, "lat", None, None),
            P(),
            P(),
        ),
        out_specs=(
            P(),
            P("member", "lat", None, None),
            P("member", "lat", None, None),
            P("member", None),
            P(),
            P(),
            P(),
            P(),
            P(),
        ),
        check_vma=False,
    )
```
